128 devices in a mesh: zone: 4 (over z), rank: 32 (over y, x, core).
Axes of the slice: x: 4, y: 4, z: 4, core: 2. Of those that a mesh axis runs over, the one named last changes fastest.
Arguments:
- adjoint_rhs: float32 [40, 32768], P(None, ('zone', 'rank'))
- diag_blocks: float32 [40, 40, 32768], P(None, None, ('zone', 'rank'))
- precond: float32 [40, 40, 32768], P(None, None, ('zone', 'rank'))
- face_blocks: float32 [6, 40, 40, 32768], P(None, None, None, ('zone', 'rank')), may hold values from -0.625 to 0.625
- face_nbrs: int32 [6, 32768], P(None, ('zone', 'rank')), may hold values from 0 to 383, as said below
- stash_blocks: float32 [1600, 65536], P(None, ('zone', 'rank')), may hold values from -0.625 to 0.625
- stash_rows: int32 [65536], P(('zone', 'rank')), may hold values from 0 to 255
- stash_cols: int32 [65536], P(('zone', 'rank')), may hold values from 0 to 255
- stash_counts: int32 [16384], P(('zone', 'rank')), may hold values from 0 to 4, as said below
Outputs:
- adjoint: float32 [40, 32768], P(None, ('zone', 'rank'))
- residual: float32 [40, 32768], P(None, ('zone', 'rank'))
The draws below stay inside these ranges and needn't reach their ends.
Inputs may be any that keep to these rules, and one draw needn't show every extreme that they name: `stash_counts`: some device receives 4 live slots from every device; the devices that receive this many are drawn from the seed. `face_nbrs`: every device has a face neighbour at position 0 and one at the last position.
All inputs are finite; a program needn't handle non-finite values.
Results may differ from the reference program's by a relative error of at most 0.0001.
Values sent between devices are 32-bit elements; how exact they have to be, the bound alone decides.
A program may use at most 128 MiB of HBM per device.

```python
import jax
import jax.numpy as jnp
from jax import lax

BLOCK = 40
FACES = 6
E_DEV = 256
CAP = 4
ARNOLDI = 2
RIM = 64
ELEMS = 32768
SLOTS_DEV = 512
SLOTS = 65536
N_ZONE = 4
N_RANK = 32


def eye_blocks():
    places = jnp.arange(BLOCK)
    return (places[:, None] == places[None, :]).astype(jnp.float32)[:, :, None]


def block_noise(key):
    return jax.random.normal(key, (BLOCK, BLOCK, ELEMS), jnp.float32)


def draw_adjoint_rhs(key, part):
    key = jax.random.fold_in(key, 3)
    value_key, scale_key = jax.random.split(key)
    element = jnp.arange(ELEMS, dtype=jnp.float32)
    rise = 1.0 + 2.0 * element / ELEMS
    scale = jnp.exp(jax.random.uniform(scale_key, (1, ELEMS), jnp.float32, -1.2, 1.2)) * rise
    values = jax.random.normal(value_key, (BLOCK, ELEMS), jnp.float32)
    return values * scale


def draw_diag_blocks(key, part):
    key = jax.random.fold_in(key, 7)
    return 2.0 * eye_blocks() + block_noise(key) * BLOCK ** (-0.5)


def draw_precond(key, part):
    key = jax.random.fold_in(key, 9)
    return 0.5 * eye_blocks() + 0.25 * block_noise(key) * BLOCK ** (-0.5)


def draw_face_nbrs(key, part):
    key = jax.random.fold_in(key, 5)
    kind_key, own_key, rim_key = jax.random.split(key, 3)
    shape = (FACES, ELEMS)
    kind = jax.random.randint(kind_key, shape, 0, 4)
    owned = RIM + jax.random.randint(own_key, shape, 0, E_DEV)
    edge = jax.random.randint(rim_key, shape, 0, RIM)
    nbrs = jnp.where(kind == 0, edge, jnp.where(kind == 1, RIM + E_DEV + edge, owned))
    local = jnp.arange(ELEMS) % E_DEV
    first = jnp.arange(FACES)[:, None] == 0
    nbrs = jnp.where(first & (local == 0)[None, :], 0, nbrs)
    nbrs = jnp.where(first & (local == 1)[None, :], E_DEV + 2 * RIM - 1, nbrs)
    return nbrs.astype(jnp.int32)


def draw_stash_counts(key, part):
    key = jax.random.fold_in(key, 11)
    devices = N_ZONE * N_RANK
    pick_key, spread_key, fixed_key = jax.random.split(key, 3)
    busy = jax.random.randint(pick_key, (devices,), 0, 8) == 0
    chosen = jax.random.randint(fixed_key, (), 0, devices)
    busy = busy | (jnp.arange(devices) == chosen)
    light = jax.random.randint(spread_key, (devices, devices), 0, CAP // 2 + 1)
    counts = jnp.where(busy[None, :], CAP, light)
    return counts.reshape(-1).astype(jnp.int32)


def plant(drawn, key, least, high):
    spot = [jax.random.randint(jax.random.fold_in(key, axis), (), 0, length) for axis, length in enumerate(drawn.shape)]
    widest = drawn.shape.index(max(drawn.shape))
    beside = spot[:widest] + [(spot[widest] + 1) % drawn.shape[widest]] + spot[widest + 1:]
    return drawn.at[tuple(spot)].set(least).at[tuple(beside)].set(high)


def shard_levels(key, dims, pieces, smallest, top_value):
    gain, own = 1.0, jax.random.fold_in(key, 6)
    for dim, blocks in pieces:
        heights = jnp.exp(jax.random.uniform(jax.random.fold_in(own, dim), (blocks,), jnp.float32, smallest / len(pieces), top_value / len(pieces)))
        gain = gain * jnp.repeat(heights, dims[dim] // blocks).reshape([-1 if axis == dim else 1 for axis in range(len(dims))])
    return gain


def scatter_about(rng, shape, spread, bound, cuts=(), held_as=jnp.bfloat16):
    drawn = spread * jax.random.normal(rng, shape, jnp.float32)
    if cuts:
        drawn = drawn * shard_levels(rng, shape, cuts, -0.22, 0.18)
    return jnp.clip(drawn, -bound, bound).astype(held_as)


def setup_inputs(seed: int = 0) -> dict:
    key_of = jax.random.split(jax.random.key(seed), 10)
    adjoint_rhs = draw_adjoint_rhs(jax.random.fold_in(key_of[9], 71), 0)
    diag_blocks = draw_diag_blocks(jax.random.fold_in(key_of[9], 71), 0)
    precond = draw_precond(jax.random.fold_in(key_of[9], 71), 0)
    face_blocks = scatter_about(key_of[3], (FACES, BLOCK, BLOCK, ELEMS), (2 * BLOCK) ** -0.5, 0.625, ((3, 128),), jnp.float32)
    face_nbrs = draw_face_nbrs(jax.random.fold_in(key_of[9], 71), 0)
    stash_blocks = scatter_about(key_of[5], (BLOCK * BLOCK, SLOTS), (2 * BLOCK) ** -0.5, 0.625, ((1, 128),), jnp.float32)
    stash_rows = plant(jax.random.randint(key_of[6], (SLOTS,), 0, E_DEV), jax.random.fold_in(key_of[6], 1), 0, E_DEV - 1).astype(jnp.int32)
    stash_cols = plant(jax.random.randint(key_of[7], (SLOTS,), 0, E_DEV), jax.random.fold_in(key_of[7], 1), 0, E_DEV - 1).astype(jnp.int32)
    stash_counts = draw_stash_counts(jax.random.fold_in(key_of[9], 71), 0)
    return {"adjoint_rhs": adjoint_rhs, "diag_blocks": diag_blocks, "precond": precond, "face_blocks": face_blocks, "face_nbrs": face_nbrs, "stash_blocks": stash_blocks, "stash_rows": stash_rows, "stash_cols": stash_cols, "stash_counts": stash_counts}


precise = lax.Precision.HIGHEST
epsilon = 1e-06

def apply_blocks(blocks, vectors):
    return jnp.einsum('ije,je->ie', blocks, vectors, precision=precise)

def solve_normal(matrix, vector):
    extent = vector.shape[0]
    matrix_rows = [matrix[position] for position in range(extent)]
    values = [vector[position] for position in range(extent)]
    for pivot_row in range(extent):
        for lower_row in range(pivot_row + 1, extent):
            factor = matrix_rows[lower_row][pivot_row] / matrix_rows[pivot_row][pivot_row]
            matrix_rows[lower_row] = matrix_rows[lower_row] - factor * matrix_rows[pivot_row]
            values[lower_row] = values[lower_row] - factor * values[pivot_row]
    answer = [None] * extent
    for pivot_row in reversed(range(extent)):
        running = values[pivot_row]
        for later_col in range(pivot_row + 1, extent):
            running = running - matrix_rows[pivot_row][later_col] * answer[later_col]
        answer[pivot_row] = running / matrix_rows[pivot_row][pivot_row]
    return jnp.stack(answer)

def face_sources(face_nbrs):
    element = jnp.arange(ELEMS, dtype=jnp.int32)
    owner = (element // E_DEV)[None, :]
    rank_of = owner % N_RANK
    prev_src = (owner - 1) * E_DEV + E_DEV - RIM + face_nbrs
    own_src = owner * E_DEV + face_nbrs - RIM
    next_src = (owner + 1) * E_DEV + face_nbrs - RIM - E_DEV
    lower = face_nbrs < RIM
    upper = face_nbrs >= RIM + E_DEV
    source = jnp.where(lower, prev_src, jnp.where(upper, next_src, own_src))
    valid = jnp.where(lower, rank_of > 0, jnp.where(upper, rank_of < N_RANK - 1, rank_of >= 0))
    source = jnp.clip(source, 0, ELEMS - 1).astype(jnp.int32)
    return (source, valid.astype(jnp.float32))

def stash_layout(stash_blocks, stash_rows, stash_cols, stash_counts):
    devices = N_ZONE * N_RANK
    slot = jnp.arange(SLOTS, dtype=jnp.int32)
    source = slot // SLOTS_DEV
    within = slot % SLOTS_DEV
    target = within // CAP
    live = within % CAP < stash_counts[source * devices + target]
    row_global = (source * E_DEV + stash_rows).astype(jnp.int32)
    col_global = (target * E_DEV + stash_cols).astype(jnp.int32)
    blocks = (stash_blocks * live.astype(jnp.float32)[None, :]).reshape(BLOCK, BLOCK, SLOTS)
    return (row_global, col_global, blocks)

def reference(adjoint_rhs, diag_blocks, precond, face_blocks, face_nbrs, stash_blocks, stash_rows, stash_cols, stash_counts):
    source, valid = face_sources(face_nbrs)
    row_global, col_global, live_blocks = stash_layout(stash_blocks, stash_rows, stash_cols, stash_counts)

    def operate(search):
        image = apply_blocks(diag_blocks, search)
        nearby = search[:, source] * valid[None, :, :]
        image = image + jnp.einsum('fije,jfe->ie', face_blocks, nearby, precision=precise)
        coupled = jnp.einsum('ijs,is->js', live_blocks, search[:, row_global], precision=precise)
        return image.at[:, col_global].add(coupled)
    beta = jnp.sqrt(jnp.sum(adjoint_rhs * adjoint_rhs) + epsilon)
    basis = [adjoint_rhs / beta]
    searches = []
    hessen = jnp.zeros((ARNOLDI + 1, ARNOLDI), jnp.float32)
    for column in range(ARNOLDI):
        search = apply_blocks(precond, basis[column])
        searches.append(search)
        work = operate(search)
        for earlier in range(column + 1):
            product = jnp.sum(work * basis[earlier])
            hessen = hessen.at[earlier, column].set(product)
            work = work - product * basis[earlier]
        length = jnp.sqrt(jnp.sum(work * work) + epsilon)
        hessen = hessen.at[column + 1, column].set(length)
        basis.append(work / length)
    normal = jnp.dot(hessen.T, hessen, precision=precise)
    coeffs = solve_normal(normal, beta * hessen[0])
    misfit = -jnp.dot(hessen, coeffs, precision=precise)
    misfit = misfit.at[0].add(beta)
    adjoint = searches[0] * coeffs[0]
    for column in range(1, ARNOLDI):
        adjoint = adjoint + searches[column] * coeffs[column]
    residual = basis[0] * misfit[0]
    for column in range(1, ARNOLDI + 1):
        residual = residual + basis[column] * misfit[column]
    return (adjoint, residual)
```

```python
import jax
import jax.numpy as jnp
from jax import lax
from jax.experimental import pallas as pl
from jax.experimental.pallas import tpu as pltpu
from jax.sharding import PartitionSpec as P

B = 40
TILES = B // 8
LANES = 128
ZONES, RANKS = 4, 32
DEVICES = ZONES * RANKS
CAP = 4
EPS = 1e-6
DOWN = 2.0**-40
UP = 2.0**40
MESH = pl.DeviceIdType.MESH
F32 = jnp.float32

HOPS = (0, 1, 2, 1)
OFFSETS = sorted(
    ((dz, dy, dx, dc) for dz in range(4) for dy in range(4) for dx in range(4) for dc in range(2)),
    key=lambda o: (o != (0, 0, 0, 0), -(HOPS[o[0]] + HOPS[o[1]] + HOPS[o[2]])),
)


def gather_lanes(tile, index):
    return jnp.take_along_axis(tile, index, axis=1)


def total(value):
    return jnp.sum(jnp.sum(value, axis=0, keepdims=True), axis=1, keepdims=True)


def kernel(
    rhs_hbm, diag_hbm, precond_hbm, face_hbm, nbrs_hbm, stash_hbm, rows_hbm, cols_hbm, counts_hbm,
    out_ref,
    rhs, precond, blocks, stash, nbrs, rows, cols, counts,
    near, halo_out, halo_in, search0, image, sending,
    send, arrived, onehot, dots, dots_in,
    load_sem, own_sem, send_sem, recv_sem, halo_send_sem, halo_recv_sem,
):
    zone, rank = lax.axis_index("zone"), lax.axis_index("rank")
    y, x, core = rank // 8, (rank // 2) % 4, rank % 2
    me = zone * RANKS + rank
    zs = [(zone + d) % 4 for d in range(4)]
    ys = [((y + d) % 4) * 8 for d in range(4)]
    xs = [((x + d) % 4) * 2 for d in range(4)]
    cs = [(core + d) % 2 for d in range(2)]
    yxs = [[ys[a] + xs[b] for b in range(4)] for a in range(4)]

    def place(offset):
        dz, dy, dx, dc = offset
        return zs[dz], yxs[dy][dx] + cs[dc]

    small = [
        pltpu.make_async_copy(rhs_hbm, rhs, load_sem.at[0]),
        pltpu.make_async_copy(rows_hbm, rows, load_sem.at[1]),
        pltpu.make_async_copy(counts_hbm, counts, load_sem.at[2]),
        pltpu.make_async_copy(cols_hbm, cols, load_sem.at[3]),
        pltpu.make_async_copy(nbrs_hbm, nbrs, load_sem.at[4]),
    ]
    load_precond = pltpu.make_async_copy(precond_hbm, precond, load_sem.at[5])
    load_stash = [
        pltpu.make_async_copy(
            stash_hbm.at[:, pl.ds(c * LANES, LANES)], stash.at[c], load_sem.at[6 + c]
        )
        for c in range(4)
    ]
    load_diag = pltpu.make_async_copy(diag_hbm, blocks.at[0], load_sem.at[10])
    load_face = pltpu.make_async_copy(face_hbm, blocks.at[pl.ds(1, 6)], load_sem.at[11])
    for load in [*small, load_precond, *load_stash, load_diag, load_face]:
        load.start()

    barrier = pltpu.get_barrier_semaphore()
    for offset in OFFSETS[1:]:
        pl.semaphore_signal(barrier, inc=1, device_id=place(offset), device_id_type=MESH)

    lane = lax.broadcasted_iota(jnp.int32, (8, LANES), 1)
    sub = lax.broadcasted_iota(jnp.int32, (8, LANES), 0)
    left = lane < LANES // 2
    pair = 2 * (lane % (LANES // 2))

    def halos(step):
        return (
            pltpu.make_async_remote_copy(
                src_ref=halo_out.at[step, 1], dst_ref=halo_in.at[step, 0],
                send_sem=halo_send_sem.at[step, 0], recv_sem=halo_recv_sem.at[step, 0],
                device_id=(zone, rank + 1), device_id_type=MESH,
            ),
            pltpu.make_async_remote_copy(
                src_ref=halo_out.at[step, 0], dst_ref=halo_in.at[step, 1],
                send_sem=halo_send_sem.at[step, 1], recv_sem=halo_recv_sem.at[step, 1],
                device_id=(zone, rank - 1), device_id_type=MESH,
            ),
        )

    def start_halos(step):
        up, down = halos(step)

        @pl.when(rank < RANKS - 1)
        def _():
            up.start()

        @pl.when(rank > 0)
        def _():
            down.start()

    def wait_halos(step):
        up, down = halos(step)

        @pl.when(rank > 0)
        def _():
            up.wait_recv()

        @pl.when(rank == 0)
        def _():
            halo_in[step, 0] = jnp.zeros((B, LANES), F32)

        @pl.when(rank < RANKS - 1)
        def _():
            down.wait_recv()

        @pl.when(rank == RANKS - 1)
        def _():
            halo_in[step, 1] = jnp.zeros((B, LANES), F32)

        @pl.when(rank < RANKS - 1)
        def _():
            up.wait_send()

        @pl.when(rank > 0)
        def _():
            down.wait_send()

    def apply_precond(step):
        def rows_of(block, _):
            first = pl.multiple_of(block * 8, 8)
            acc = None
            for t in range(TILES):
                term = precond[pl.ds(first, 8), t * 8 : t * 8 + 8, :] * near[0, t * 8 : t * 8 + 8, :][None]
                acc = term if acc is None else acc + term
            product = jnp.sum(acc, axis=1)
            halo_out[step, 0, pl.ds(first, 8), :] = product[:, :LANES]
            halo_out[step, 1, pl.ds(first, 8), :] = product[:, LANES:]
            return 0

        lax.fori_loop(0, TILES, rows_of, 0)

    def expand_counts(c):
        tile = jnp.broadcast_to(counts[...], (8, LANES))
        return gather_lanes(tile, c * 32 + lane // CAP)

    def gather_sending(step, c):
        at = jnp.broadcast_to(rows[c : c + 1, :], (8, LANES))
        live = jnp.where(lane % CAP < expand_counts(c), 1.0, 0.0)
        low, at = at < LANES, at % LANES
        for t in range(TILES):
            first = gather_lanes(halo_out[step, 0, t * 8 : t * 8 + 8, :], at)
            second = gather_lanes(halo_out[step, 1, t * 8 : t * 8 + 8, :], at)
            sending[c, t * 8 : t * 8 + 8, :] = jnp.where(low, first, second) * live

    def couple(c):
        def step_of(i, acc):
            row = pl.multiple_of(i * B, 8)
            factor = jnp.broadcast_to(sending[c, pl.ds(i, 1), :], (8, LANES))
            return tuple(acc[t] + stash[c, pl.ds(row + t * 8, 8), :] * factor for t in range(TILES))

        zero = jnp.zeros((8, LANES), F32)
        return lax.fori_loop(0, B, step_of, (zero,) * TILES, unroll=8)

    def pack(step, p, couplings, scalars):
        zero = jnp.zeros((8, LANES), F32)
        tiles = []
        for h in range(2):
            for t in range(TILES):
                first = gather_lanes(couplings[0][t], pair + h)
                second = gather_lanes(couplings[1][t], pair + h)
                tiles.append(jnp.where(left, first, second))
            first = gather_lanes(jnp.broadcast_to(cols[2 * p : 2 * p + 1, :], (8, LANES)), pair + h)
            second = gather_lanes(jnp.broadcast_to(cols[2 * p + 1 : 2 * p + 2, :], (8, LANES)), pair + h)
            extra = jnp.where(sub == 0, jnp.where(left, first, second).astype(F32), 0.0)
            for place_of, scalar in enumerate(scalars):
                extra = jnp.where(sub == 1 + place_of, scalar, extra)
            tiles += [extra, zero, zero]
        turned = jnp.concatenate(tiles, axis=0).T
        for d in range(64):
            send[step, 64 * p + d] = turned[2 * d : 2 * d + 2, :]

    def message(step, place_of):
        z, r = place(OFFSETS[place_of])
        return pltpu.make_async_remote_copy(
            src_ref=send.at[step, z * RANKS + r], dst_ref=arrived.at[step, place_of],
            send_sem=send_sem.at[step], recv_sem=recv_sem.at[step],
            device_id=(z, r), device_id_type=MESH,
        )

    def own(step):
        return pltpu.make_async_copy(send.at[step, me], arrived.at[step, 0], own_sem.at[step])

    def all_arrived(step):
        others = arrived.at[step, pl.ds(1, DEVICES - 1)]
        pltpu.make_async_copy(others, others, recv_sem.at[step]).wait()
        own(step).wait()

    def exchange(step, scalars):
        for c in range(4):
            if step == 0:
                load_stash[c].wait()
            gather_sending(step, c)
        for p in range(2):
            pack(step, p, (couple(2 * p), couple(2 * p + 1)), scalars)
        own(step).start()
        for place_of in range(1, DEVICES):
            message(step, place_of).start()

    def apply_local(step):
        for t in range(TILES):
            tile = slice(t * 8, t * 8 + 8)
            zero_tile = halo_out[step, 0, tile, :]
            one_tile = halo_out[step, 1, tile, :]
            rim_tile = jnp.where(left, halo_in[step, 1, tile, :], halo_in[step, 0, tile, :])
            near[0, tile, :LANES] = zero_tile
            near[0, tile, LANES:] = one_tile
            for f in range(6):
                for c in range(2):
                    at = jnp.broadcast_to(nbrs[f : f + 1, c * LANES : c * LANES + LANES], (8, LANES))
                    index = (at + 64) % LANES
                    found = jnp.where(
                        (at >= 64) & (at < 192), gather_lanes(zero_tile, index),
                        jnp.where((at >= 192) & (at < 320), gather_lanes(one_tile, index), gather_lanes(rim_tile, index)),
                    )
                    near[1 + f, tile, c * LANES : c * LANES + LANES] = found
        if step == 0:
            load_diag.wait()
            load_face.wait()

        def rows_of(block, _):
            first = pl.multiple_of(block * 8, 8)
            acc = None
            for b in range(7):
                for t in range(TILES):
                    term = blocks[b, pl.ds(first, 8), t * 8 : t * 8 + 8, :] * near[b, t * 8 : t * 8 + 8, :][None]
                    acc = term if acc is None else acc + term
            image[pl.ds(first, 8), :] = jnp.sum(acc, axis=1)
            return 0

        lax.fori_loop(0, TILES, rows_of, 0)

    def received(step):
        return jnp.concatenate([arrived[step, k] for k in range(DEVICES)], axis=0)

    def scattered(table):
        turned = table.T
        halves = []
        for h in range(2):
            rest = turned[64 * h : 64 * h + 48, :]
            parts = []
            for _ in range(3):
                part = rest.astype(jnp.bfloat16)
                parts.append(part)
                rest = rest - part.astype(F32)
            halves.append(jnp.concatenate(parts, axis=0))
        product = jnp.dot(jnp.concatenate(halves, axis=1), onehot[...], preferred_element_type=F32)
        return product[:B] + product[48 : 48 + B] + product[96 : 96 + B]

    small[0].wait()
    near[0] = rhs[...] * DOWN
    square = total(rhs[...] * rhs[...])
    load_precond.wait()
    apply_precond(0)
    small[1].wait()
    small[2].wait()
    small[3].wait()
    small[4].wait()
    pl.semaphore_wait(barrier, DEVICES - 1)
    start_halos(0)
    exchange(0, (square,))
    wait_halos(0)
    apply_local(0)
    all_arrived(0)
    table = received(0)
    element = lax.broadcasted_iota(jnp.int32, (256, 256), 1).astype(F32)
    for h in range(2):
        column = table[:, 64 * h + B : 64 * h + B + 1]
        onehot[256 * h : 256 * h + 256, :] = jnp.where(element == column, 1.0, 0.0).astype(jnp.bfloat16)
    sums = jnp.sum(table, axis=0, keepdims=True) * 0.5
    square = sums[:, B + 1 : B + 2]
    beta = jnp.sqrt(square + EPS)
    basis0 = rhs[...] / beta
    factor = UP / beta
    work0 = (image[...] + scattered(table)) * factor
    search0[:, :LANES] = halo_out[0, 0] * factor
    search0[:, LANES:] = halo_out[0, 1] * factor

    near[0] = work0
    apply_precond(1)
    start_halos(1)
    exchange(1, (total(work0 * basis0), total(work0 * work0)))
    wait_halos(1)
    apply_local(1)
    all_arrived(1)
    table = received(1)
    sums = jnp.sum(table, axis=0, keepdims=True) * 0.5
    h00 = sums[:, B + 1 : B + 2]
    size = jnp.sqrt(sums[:, B + 2 : B + 3] + EPS)
    work1 = work0 - h00 * basis0
    second = (image[...] + scattered(table) - h00 * work0) / size

    values = (
        total(work1 * work1), total(work1 * basis0), total(second * basis0), total(second * work1), total(second * second)
    )
    row_lane = lax.broadcasted_iota(jnp.int32, (1, LANES), 1)
    mine = jnp.zeros((1, LANES), F32)
    for place_of, value in enumerate(values):
        mine = jnp.where(row_lane == place_of, value, mine)
    dots[...] = mine
    dots_in[0] = mine

    def tell(place_of):
        return pltpu.make_async_remote_copy(
            src_ref=dots, dst_ref=dots_in.at[place_of], send_sem=send_sem.at[2], recv_sem=recv_sem.at[2],
            device_id=place(OFFSETS[place_of]), device_id_type=MESH,
        )

    for place_of in range(1, DEVICES):
        tell(place_of).start()
    others = dots_in.at[pl.ds(1, DEVICES - 1)]
    pltpu.make_async_copy(others, others, recv_sem.at[2]).wait()
    sums = jnp.sum(dots_in[...], axis=0)
    n1, cross, a, b, d = (sums[:, k : k + 1] for k in range(5))
    h10 = jnp.sqrt(n1 + EPS)
    ratio = size / h10
    h01 = ratio * a
    along = ratio * b / h10
    skew = cross / h10
    h11 = along - h01 * skew
    unit = square / (square + EPS)
    left_over = (
        ratio * ratio * d - 2.0 * h01 * h01 + unit * h01 * h01
        - 2.0 * h11 * along + h11 * h11 * n1 / (h10 * h10) + 2.0 * h01 * h11 * skew
    )
    n00 = h00 * h00 + h10 * h10
    n01 = h00 * h01 + h10 * h11
    n11 = h01 * h01 + h11 * h11 + (jnp.maximum(left_over, 0.0) + EPS)
    lower = n01 / n00
    c1 = (beta * h01 - lower * (beta * h00)) / (n11 - lower * n01)
    c0 = (beta * h00 - n01 * c1) / n00
    mixed = c1 / h10
    for c in range(2):
        half = slice(c * LANES, c * LANES + LANES)
        out_ref[0, :, half] = (c0 - mixed * h00) * search0[:, half] + mixed * halo_out[1, c]
    out_ref[1] = rhs[...] - c0 * work0 - (c1 * ratio) * second

    for step in range(2):
        others = arrived.at[step, pl.ds(1, DEVICES - 1)]
        pltpu.make_async_copy(others, others, send_sem.at[step]).wait()
    others = dots_in.at[pl.ds(1, DEVICES - 1)]
    pltpu.make_async_copy(others, others, send_sem.at[2]).wait()


def per_device(rhs, diag, precond, face, nbrs, stash, rows, cols, counts):
    anywhere = pl.BlockSpec(memory_space=pl.ANY)
    out = pl.pallas_call(
        kernel,
        out_shape=jax.ShapeDtypeStruct((2, B, 256), F32),
        in_specs=[anywhere] * 9,
        out_specs=pl.BlockSpec(memory_space=pltpu.VMEM),
        scratch_shapes=[
            pltpu.VMEM((B, 256), F32),
            pltpu.VMEM((B, B, 256), F32),
            pltpu.VMEM((7, B, B, 256), F32),
            pltpu.VMEM((4, B * B, LANES), F32),
            pltpu.VMEM((6, 256), jnp.int32),
            pltpu.VMEM((4, LANES), jnp.int32),
            pltpu.VMEM((4, LANES), jnp.int32),
            pltpu.VMEM((1, LANES), jnp.int32),
            pltpu.VMEM((7, B, 256), F32),
            pltpu.VMEM((2, 2, B, LANES), F32),
            pltpu.VMEM((2, 2, B, LANES), F32),
            pltpu.VMEM((B, 256), F32),
            pltpu.VMEM((B, 256), F32),
            pltpu.VMEM((4, B, LANES), F32),
            pltpu.VMEM((2, DEVICES, 2, LANES), F32),
            pltpu.VMEM((2, DEVICES, 2, LANES), F32),
            pltpu.VMEM((512, 256), jnp.bfloat16),
            pltpu.VMEM((1, LANES), F32),
            pltpu.VMEM((DEVICES, 1, LANES), F32),
            pltpu.SemaphoreType.DMA((12,)),
            pltpu.SemaphoreType.DMA((2,)),
            pltpu.SemaphoreType.DMA((3,)),
            pltpu.SemaphoreType.DMA((3,)),
            pltpu.SemaphoreType.DMA((2, 2)),
            pltpu.SemaphoreType.DMA((2, 2)),
        ],
        compiler_params=pltpu.CompilerParams(
            collective_id=0, has_side_effects=True, vmem_limit_bytes=48 * 2**20
        ),
        name="gmres",
    )(rhs, diag, precond, face, nbrs, stash, rows.reshape(4, LANES), cols.reshape(4, LANES), counts.reshape(1, LANES))
    return out[0], out[1]


def solution(mesh):
    spread = ("zone", "rank")
    return jax.shard_map(
        per_device,
        mesh=mesh,
        in_specs=(
            P(None, spread),
            P(None, None, spread),
            P(None, None, spread),
            P(None, None, None, spread),
            P(None, spread),
            P(None, spread),
            P(spread),
            P(spread),
            P(spread),
        ),
        out_specs=(P(None, spread), P(None, spread)),
        check_vma=False,
    )
```

```python
import jax
import jax.numpy as jnp
from jax import lax
from jax.experimental import pallas as pl
from jax.experimental.pallas import tpu as pltpu
from jax.sharding import PartitionSpec as P

B = 40
TILES = B // 8
LANES = 128
ZONES, RANKS = 4, 32
DEVICES = ZONES * RANKS
CAP = 4
EPS = 1e-6
DOWN = 2.0**-40
UP = 2.0**40
MESH = pl.DeviceIdType.MESH
F32 = jnp.float32

HOPS = (0, 1, 2, 1)
PLANE = [(dy, dx, dc) for dy in range(4) for dx in range(4) for dc in range(2)]


def plane_hops(offset):
    return HOPS[offset[0]] + HOPS[offset[1]]


OTHERS = sorted(
    ((dz, offset) for dz in range(4) for offset in PLANE if dz or any(offset)),
    key=lambda other: -(HOPS[other[0]] + plane_hops(other[1])),
)
KINDS = sorted(
    ((kind, offset) for kind in (2, 1, -1, 0) for offset in PLANE if kind or any(offset)),
    key=lambda other: -(abs(other[0]) + plane_hops(other[1])),
)


def gather_lanes(tile, index):
    return jnp.take_along_axis(tile, index, axis=1)


def total(value):
    return jnp.sum(jnp.sum(value, axis=0, keepdims=True), axis=1, keepdims=True)


def kernel(
    rhs_hbm, diag_hbm, precond_hbm, face_hbm, nbrs_hbm, stash_hbm, rows_hbm, cols_hbm, counts_hbm,
    out_ref,
    rhs, precond, blocks, stash, nbrs, rows, cols, counts,
    near, halo_out, halo_in, search0, image, sending,
    send, arrived, onehot, dots, dots_in,
    load_sem, own_sem, send_sem, recv_sem, halo_send_sem, halo_recv_sem,
):
    zone, rank = lax.axis_index("zone"), lax.axis_index("rank")
    y, x, core = rank // 8, (rank // 2) % 4, rank % 2
    me = zone * RANKS + rank
    zs = [(zone + d) % 4 for d in range(4)]
    ys = [((y + d) % 4) * 8 for d in range(4)]
    xs = [((x + d) % 4) * 2 for d in range(4)]
    cs = [(core + d) % 2 for d in range(2)]
    yxs = [[ys[a] + xs[b] for b in range(4)] for a in range(4)]

    def rank_at(offset):
        dy, dx, dc = offset
        return yxs[dy][dx] + cs[dc]

    def place(other):
        return zs[other[0]], rank_at(other[1])

    mate = 3 - 2 * (zone % 2)
    ahead = {2: 2, 1: mate, -1: 4 - mate, 0: 0}
    far_pair = ((zone + 2) % 4) // 2
    pairs = (far_pair, 1 - far_pair)
    chunks = tuple(2 * p + k for p in pairs for k in range(2))

    barrier = pltpu.get_barrier_semaphore()

    def greet(others):
        for other in others:
            pl.semaphore_signal(barrier, inc=1, device_id=place(other), device_id_type=MESH)

    greet(OTHERS[:44])

    small = [
        pltpu.make_async_copy(rhs_hbm, rhs, load_sem.at[0]),
        pltpu.make_async_copy(rows_hbm, rows, load_sem.at[1]),
        pltpu.make_async_copy(counts_hbm, counts, load_sem.at[2]),
        pltpu.make_async_copy(cols_hbm, cols, load_sem.at[3]),
        pltpu.make_async_copy(nbrs_hbm, nbrs, load_sem.at[4]),
    ]
    load_precond = pltpu.make_async_copy(precond_hbm, precond, load_sem.at[5])
    load_stash = [
        pltpu.make_async_copy(
            stash_hbm.at[:, pl.ds(pl.multiple_of(c * LANES, LANES), LANES)], stash.at[c], load_sem.at[6 + k]
        )
        for k, c in enumerate(chunks)
    ]
    load_diag = pltpu.make_async_copy(diag_hbm, blocks.at[0], load_sem.at[10])
    load_face = pltpu.make_async_copy(face_hbm, blocks.at[pl.ds(1, 6)], load_sem.at[11])
    for load in [*small, load_precond, *load_stash, load_diag, load_face]:
        load.start()
    greet(OTHERS[44:])

    lane = lax.broadcasted_iota(jnp.int32, (8, LANES), 1)
    sub = lax.broadcasted_iota(jnp.int32, (8, LANES), 0)
    left = lane < LANES // 2
    pair = 2 * (lane % (LANES // 2))

    def halos(step):
        return (
            pltpu.make_async_remote_copy(
                src_ref=halo_out.at[step, 1], dst_ref=halo_in.at[step, 0],
                send_sem=halo_send_sem.at[step, 0], recv_sem=halo_recv_sem.at[step, 0],
                device_id=(zone, rank + 1), device_id_type=MESH,
            ),
            pltpu.make_async_remote_copy(
                src_ref=halo_out.at[step, 0], dst_ref=halo_in.at[step, 1],
                send_sem=halo_send_sem.at[step, 1], recv_sem=halo_recv_sem.at[step, 1],
                device_id=(zone, rank - 1), device_id_type=MESH,
            ),
        )

    def start_halos(step):
        up, down = halos(step)

        @pl.when(rank < RANKS - 1)
        def _():
            up.start()

        @pl.when(rank > 0)
        def _():
            down.start()

    def wait_halos(step):
        up, down = halos(step)

        @pl.when(rank > 0)
        def _():
            up.wait_recv()

        @pl.when(rank == 0)
        def _():
            halo_in[step, 0] = jnp.zeros((B, LANES), F32)

        @pl.when(rank < RANKS - 1)
        def _():
            down.wait_recv()

        @pl.when(rank == RANKS - 1)
        def _():
            halo_in[step, 1] = jnp.zeros((B, LANES), F32)

        @pl.when(rank < RANKS - 1)
        def _():
            up.wait_send()

        @pl.when(rank > 0)
        def _():
            down.wait_send()

    def apply_precond(step):
        def rows_of(block, _):
            first = pl.multiple_of(block * 8, 8)
            acc = None
            for t in range(TILES):
                term = precond[pl.ds(first, 8), t * 8 : t * 8 + 8, :] * near[0, t * 8 : t * 8 + 8, :][None]
                acc = term if acc is None else acc + term
            product = jnp.sum(acc, axis=1)
            halo_out[step, 0, pl.ds(first, 8), :] = product[:, :LANES]
            halo_out[step, 1, pl.ds(first, 8), :] = product[:, LANES:]
            return 0

        lax.fori_loop(0, TILES, rows_of, 0)

    def expand_counts(c):
        tile = jnp.broadcast_to(counts[...], (8, LANES))
        return gather_lanes(tile, c * 32 + lane // CAP)

    def gather_sending(step, c):
        at = jnp.broadcast_to(rows[pl.ds(c, 1), :], (8, LANES))
        live = jnp.where(lane % CAP < expand_counts(c), 1.0, 0.0)
        low, at = at < LANES, at % LANES
        for t in range(TILES):
            first = gather_lanes(halo_out[step, 0, t * 8 : t * 8 + 8, :], at)
            second = gather_lanes(halo_out[step, 1, t * 8 : t * 8 + 8, :], at)
            sending[c, t * 8 : t * 8 + 8, :] = jnp.where(low, first, second) * live

    def couple(pair_of):
        def step_of(i, acc):
            row = pl.multiple_of(i * B, 8)
            added = []
            for c in pair_of:
                factor = jnp.broadcast_to(sending[c, pl.ds(i, 1), :], (8, LANES))
                added += [stash[c, pl.ds(row + t * 8, 8), :] * factor for t in range(TILES)]
            return tuple(old + new for old, new in zip(acc, added))

        zero = jnp.zeros((8, LANES), F32)
        sums = lax.fori_loop(0, B, step_of, (zero,) * (2 * TILES), unroll=8)
        return sums[:TILES], sums[TILES:]

    def pack(step, p, couplings, scalars):
        zero = jnp.zeros((8, LANES), F32)
        tiles = []
        for h in range(2):
            for t in range(TILES):
                first = gather_lanes(couplings[0][t], pair + h)
                second = gather_lanes(couplings[1][t], pair + h)
                tiles.append(jnp.where(left, first, second))
            first = gather_lanes(jnp.broadcast_to(cols[pl.ds(2 * p, 1), :], (8, LANES)), pair + h)
            second = gather_lanes(jnp.broadcast_to(cols[pl.ds(2 * p + 1, 1), :], (8, LANES)), pair + h)
            extra = jnp.where(sub == 0, jnp.where(left, first, second).astype(F32), 0.0)
            for place_of, scalar in enumerate(scalars):
                extra = jnp.where(sub == 1 + place_of, scalar, extra)
            tiles += [extra, zero, zero]
        turned = jnp.concatenate(tiles, axis=0).T
        for d in range(64):
            send[step, 64 * p + d] = turned[2 * d : 2 * d + 2, :]

    def message(step, kind, offset):
        z, r = (zone + ahead[kind]) % 4, rank_at(offset)
        spot = offset[0] * 8 + offset[1] * 2 + offset[2]
        return pltpu.make_async_remote_copy(
            src_ref=send.at[step, z * RANKS + r], dst_ref=arrived.at[step, ahead[kind] * RANKS + spot],
            send_sem=send_sem.at[step], recv_sem=recv_sem.at[step],
            device_id=(z, r), device_id_type=MESH,
        )

    def own(step):
        return pltpu.make_async_copy(send.at[step, me], arrived.at[step, 0], own_sem.at[step])

    def all_arrived(step):
        others = arrived.at[step, pl.ds(1, DEVICES - 1)]
        pltpu.make_async_copy(others, others, recv_sem.at[step]).wait()
        own(step).wait()

    def prepare(step, k, scalars):
        pair_of = chunks[2 * k : 2 * k + 2]
        for j, c in enumerate(pair_of):
            if step == 0:
                load_stash[2 * k + j].wait()
            gather_sending(step, c)
        pack(step, pairs[k], couple(pair_of), scalars)

    def first_out(other):
        return other[0] > 0 and other[0] + plane_hops(other[1]) >= 4

    def post(step, first):
        for other in KINDS:
            if first_out(other) == first:
                message(step, *other).start()

    def apply_local(step):
        for t in range(TILES):
            tile = slice(t * 8, t * 8 + 8)
            zero_tile = halo_out[step, 0, tile, :]
            one_tile = halo_out[step, 1, tile, :]
            rim_tile = jnp.where(left, halo_in[step, 1, tile, :], halo_in[step, 0, tile, :])
            near[0, tile, :LANES] = zero_tile
            near[0, tile, LANES:] = one_tile
            for f in range(6):
                for c in range(2):
                    at = jnp.broadcast_to(nbrs[f : f + 1, c * LANES : c * LANES + LANES], (8, LANES))
                    index = (at + 64) % LANES
                    found = jnp.where(
                        (at >= 64) & (at < 192), gather_lanes(zero_tile, index),
                        jnp.where((at >= 192) & (at < 320), gather_lanes(one_tile, index), gather_lanes(rim_tile, index)),
                    )
                    near[1 + f, tile, c * LANES : c * LANES + LANES] = found
        if step == 0:
            load_diag.wait()
            load_face.wait()

        def rows_of(block, _):
            first = pl.multiple_of(block * 8, 8)
            acc = None
            for b in range(7):
                for t in range(TILES):
                    term = blocks[b, pl.ds(first, 8), t * 8 : t * 8 + 8, :] * near[b, t * 8 : t * 8 + 8, :][None]
                    acc = term if acc is None else acc + term
            image[pl.ds(first, 8), :] = jnp.sum(acc, axis=1)
            return 0

        lax.fori_loop(0, TILES, rows_of, 0)

    def received(step):
        return jnp.concatenate([arrived[step, k] for k in range(DEVICES)], axis=0)

    def scattered(table):
        turned = table.T
        halves = []
        for h in range(2):
            rest = turned[64 * h : 64 * h + 48, :]
            parts = []
            for _ in range(3):
                part = rest.astype(jnp.bfloat16)
                parts.append(part)
                rest = rest - part.astype(F32)
            halves.append(jnp.concatenate(parts, axis=0))
        product = jnp.dot(jnp.concatenate(halves, axis=1), onehot[...], preferred_element_type=F32)
        return product[:B] + product[48 : 48 + B] + product[96 : 96 + B]

    small[0].wait()
    near[0] = rhs[...] * DOWN
    square = total(rhs[...] * rhs[...])
    load_precond.wait()
    apply_precond(0)
    small[1].wait()
    small[2].wait()
    small[3].wait()
    small[4].wait()
    for k in range(2):
        prepare(0, k, (square,))
    pl.semaphore_wait(barrier, DEVICES - 1)
    start_halos(0)
    post(0, True)
    post(0, False)
    own(0).start()
    wait_halos(0)
    apply_local(0)
    all_arrived(0)
    table = received(0)
    element = lax.broadcasted_iota(jnp.int32, (256, 256), 1).astype(F32)
    for h in range(2):
        column = table[:, 64 * h + B : 64 * h + B + 1]
        onehot[256 * h : 256 * h + 256, :] = jnp.where(element == column, 1.0, 0.0).astype(jnp.bfloat16)
    sums = jnp.sum(table, axis=0, keepdims=True) * 0.5
    square = sums[:, B + 1 : B + 2]
    beta = jnp.sqrt(square + EPS)
    basis0 = rhs[...] / beta
    factor = UP / beta
    work0 = (image[...] + scattered(table)) * factor
    search0[:, :LANES] = halo_out[0, 0] * factor
    search0[:, LANES:] = halo_out[0, 1] * factor

    near[0] = work0
    apply_precond(1)
    start_halos(1)
    scalars = (total(work0 * basis0), total(work0 * work0))
    prepare(1, 0, scalars)
    post(1, True)
    prepare(1, 1, scalars)
    post(1, False)
    own(1).start()
    wait_halos(1)
    apply_local(1)
    all_arrived(1)
    table = received(1)
    sums = jnp.sum(table, axis=0, keepdims=True) * 0.5
    h00 = sums[:, B + 1 : B + 2]
    size = jnp.sqrt(sums[:, B + 2 : B + 3] + EPS)
    work1 = work0 - h00 * basis0
    second = (image[...] + scattered(table) - h00 * work0) / size

    values = (
        total(work1 * work1), total(work1 * basis0), total(second * basis0), total(second * work1), total(second * second)
    )
    row_lane = lax.broadcasted_iota(jnp.int32, (1, LANES), 1)
    mine = jnp.zeros((1, LANES), F32)
    for place_of, value in enumerate(values):
        mine = jnp.where(row_lane == place_of, value, mine)
    dots[...] = mine
    dots_in[0] = mine

    def tell(other):
        dz, (dy, dx, dc) = other
        return pltpu.make_async_remote_copy(
            src_ref=dots, dst_ref=dots_in.at[dz * RANKS + dy * 8 + dx * 2 + dc],
            send_sem=send_sem.at[2], recv_sem=recv_sem.at[2],
            device_id=place(other), device_id_type=MESH,
        )

    for other in OTHERS:
        tell(other).start()
    others = dots_in.at[pl.ds(1, DEVICES - 1)]
    pltpu.make_async_copy(others, others, recv_sem.at[2]).wait()
    sums = jnp.sum(dots_in[...], axis=0)
    n1, cross, a, b, d = (sums[:, k : k + 1] for k in range(5))
    h10 = jnp.sqrt(n1 + EPS)
    ratio = size / h10
    h01 = ratio * a
    along = ratio * b / h10
    skew = cross / h10
    h11 = along - h01 * skew
    unit = square / (square + EPS)
    left_over = (
        ratio * ratio * d - 2.0 * h01 * h01 + unit * h01 * h01
        - 2.0 * h11 * along + h11 * h11 * n1 / (h10 * h10) + 2.0 * h01 * h11 * skew
    )
    n00 = h00 * h00 + h10 * h10
    n01 = h00 * h01 + h10 * h11
    n11 = h01 * h01 + h11 * h11 + (jnp.maximum(left_over, 0.0) + EPS)
    lower = n01 / n00
    c1 = (beta * h01 - lower * (beta * h00)) / (n11 - lower * n01)
    c0 = (beta * h00 - n01 * c1) / n00
    mixed = c1 / h10
    for c in range(2):
        half = slice(c * LANES, c * LANES + LANES)
        out_ref[0, :, half] = (c0 - mixed * h00) * search0[:, half] + mixed * halo_out[1, c]
    out_ref[1] = rhs[...] - c0 * work0 - (c1 * ratio) * second

    for step in range(2):
        others = arrived.at[step, pl.ds(1, DEVICES - 1)]
        pltpu.make_async_copy(others, others, send_sem.at[step]).wait()
    others = dots_in.at[pl.ds(1, DEVICES - 1)]
    pltpu.make_async_copy(others, others, send_sem.at[2]).wait()


def per_device(rhs, diag, precond, face, nbrs, stash, rows, cols, counts):
    arrays = (
        rhs, diag, precond, face, nbrs, stash, rows.reshape(4, LANES), cols.reshape(4, LANES), counts.reshape(1, LANES)
    )
    anywhere = pl.BlockSpec(memory_space=pl.ANY)
    out = pl.pallas_call(
        kernel,
        out_shape=jax.ShapeDtypeStruct((2, B, 256), F32),
        in_specs=[anywhere] * 9,
        out_specs=pl.BlockSpec(memory_space=pltpu.VMEM),
        scratch_shapes=[
            pltpu.VMEM((B, 256), F32),
            pltpu.VMEM((B, B, 256), F32),
            pltpu.VMEM((7, B, B, 256), F32),
            pltpu.VMEM((4, B * B, LANES), F32),
            pltpu.VMEM((6, 256), jnp.int32),
            pltpu.VMEM((4, LANES), jnp.int32),
            pltpu.VMEM((4, LANES), jnp.int32),
            pltpu.VMEM((1, LANES), jnp.int32),
            pltpu.VMEM((7, B, 256), F32),
            pltpu.VMEM((2, 2, B, LANES), F32),
            pltpu.VMEM((2, 2, B, LANES), F32),
            pltpu.VMEM((B, 256), F32),
            pltpu.VMEM((B, 256), F32),
            pltpu.VMEM((4, B, LANES), F32),
            pltpu.VMEM((2, DEVICES, 2, LANES), F32),
            pltpu.VMEM((2, DEVICES, 2, LANES), F32),
            pltpu.VMEM((512, 256), jnp.bfloat16),
            pltpu.VMEM((1, LANES), F32),
            pltpu.VMEM((DEVICES, 1, LANES), F32),
            pltpu.SemaphoreType.DMA((12,)),
            pltpu.SemaphoreType.DMA((2,)),
            pltpu.SemaphoreType.DMA((3,)),
            pltpu.SemaphoreType.DMA((3,)),
            pltpu.SemaphoreType.DMA((2, 2)),
            pltpu.SemaphoreType.DMA((2, 2)),
        ],
        compiler_params=pltpu.CompilerParams(
            collective_id=0, has_side_effects=True, vmem_limit_bytes=48 * 2**20
        ),
        name="gmres",
    )(*(pltpu.with_memory_space_constraint(array, pltpu.HBM) for array in arrays))
    return out[0], out[1]


def solution(mesh):
    spread = ("zone", "rank")
    return jax.shard_map(
        per_device,
        mesh=mesh,
        in_specs=(
            P(None, spread),
            P(None, None, spread),
            P(None, None, spread),
            P(None, None, None, spread),
            P(None, spread),
            P(None, spread),
            P(spread),
            P(spread),
            P(spread),
        ),
        out_specs=(P(None, spread), P(None, spread)),
        check_vma=False,
    )
```

```python
import jax
import jax.numpy as jnp
from jax import lax
from jax.experimental import pallas as pl
from jax.experimental.pallas import tpu as pltpu
from jax.sharding import PartitionSpec as P

B = 40
TILES = B // 8
LANES = 128
ZONES, RANKS = 4, 32
DEVICES = ZONES * RANKS
CAP = 4
EPS = 1e-6
DOWN = 2.0**-40
UP = 2.0**40
MESH = pl.DeviceIdType.MESH
F32 = jnp.float32

HOPS = (0, 1, 2, 1)
PLANE = [(dy, dx, dc) for dy in range(4) for dx in range(4) for dc in range(2)]


def plane_hops(offset):
    return HOPS[offset[0]] + HOPS[offset[1]]


OTHERS = sorted(
    ((dz, offset) for dz in range(4) for offset in PLANE if dz or any(offset)),
    key=lambda other: -(HOPS[other[0]] + plane_hops(other[1])),
)
KINDS = sorted(
    ((kind, offset) for kind in (2, 1, -1, 0) for offset in PLANE if kind or any(offset)),
    key=lambda other: -(abs(other[0]) + plane_hops(other[1])),
)


def gather_lanes(tile, index):
    return jnp.take_along_axis(tile, index, axis=1)


def add_up(terms):
    terms = list(terms)
    while len(terms) > 1:
        terms = [terms[k] + terms[k + 1] if k + 1 < len(terms) else terms[k] for k in range(0, len(terms), 2)]
    return terms[0]


def total(value):
    return jnp.sum(jnp.sum(value, axis=0, keepdims=True), axis=1, keepdims=True)


def kernel(
    rhs_hbm, diag_hbm, precond_hbm, face_hbm, nbrs_hbm, stash_hbm, rows_hbm, cols_hbm, counts_hbm,
    out_ref,
    rhs, precond, blocks, stash, nbrs, rows, cols, counts,
    near, halo_out, halo_in, search0, image, sending,
    send, arrived, onehot, dots, dots_in,
    load_sem, own_sem, send_sem, recv_sem, halo_send_sem, halo_recv_sem,
):
    zone, rank = lax.axis_index("zone"), lax.axis_index("rank")
    y, x, core = rank // 8, (rank // 2) % 4, rank % 2
    me = zone * RANKS + rank
    zs = [(zone + d) % 4 for d in range(4)]
    ys = [((y + d) % 4) * 8 for d in range(4)]
    xs = [((x + d) % 4) * 2 for d in range(4)]
    cs = [(core + d) % 2 for d in range(2)]
    yxs = [[ys[a] + xs[b] for b in range(4)] for a in range(4)]

    def rank_at(offset):
        dy, dx, dc = offset
        return yxs[dy][dx] + cs[dc]

    def place(other):
        return zs[other[0]], rank_at(other[1])

    mate = 3 - 2 * (zone % 2)
    ahead = {2: 2, 1: mate, -1: 4 - mate, 0: 0}
    far_pair = ((zone + 2) % 4) // 2
    pairs = (far_pair, 1 - far_pair)
    chunks = tuple(2 * p + k for p in pairs for k in range(2))

    barrier = pltpu.get_barrier_semaphore()

    def greet(others):
        for other in others:
            pl.semaphore_signal(barrier, inc=1, device_id=place(other), device_id_type=MESH)

    greet(OTHERS[:44])

    small = [
        pltpu.make_async_copy(rhs_hbm, rhs, load_sem.at[0]),
        pltpu.make_async_copy(rows_hbm, rows, load_sem.at[1]),
        pltpu.make_async_copy(counts_hbm, counts, load_sem.at[2]),
        pltpu.make_async_copy(cols_hbm, cols, load_sem.at[3]),
        pltpu.make_async_copy(nbrs_hbm, nbrs, load_sem.at[4]),
    ]
    load_precond = pltpu.make_async_copy(precond_hbm, precond, load_sem.at[5])
    load_stash = [
        pltpu.make_async_copy(
            stash_hbm.at[:, pl.ds(pl.multiple_of(c * LANES, LANES), LANES)], stash.at[c], load_sem.at[6 + k]
        )
        for k, c in enumerate(chunks)
    ]
    load_diag = pltpu.make_async_copy(diag_hbm, blocks.at[0], load_sem.at[10])
    load_face = pltpu.make_async_copy(face_hbm, blocks.at[pl.ds(1, 6)], load_sem.at[11])
    for load in [*small, load_precond, *load_stash, load_diag, load_face]:
        load.start()
    greet(OTHERS[44:])

    lane = lax.broadcasted_iota(jnp.int32, (8, LANES), 1)
    sub = lax.broadcasted_iota(jnp.int32, (8, LANES), 0)
    left = lane < LANES // 2
    pair = 2 * (lane % (LANES // 2))

    def halos(step):
        return (
            pltpu.make_async_remote_copy(
                src_ref=halo_out.at[step, 1], dst_ref=halo_in.at[step, 0],
                send_sem=halo_send_sem.at[step, 0], recv_sem=halo_recv_sem.at[step, 0],
                device_id=(zone, rank + 1), device_id_type=MESH,
            ),
            pltpu.make_async_remote_copy(
                src_ref=halo_out.at[step, 0], dst_ref=halo_in.at[step, 1],
                send_sem=halo_send_sem.at[step, 1], recv_sem=halo_recv_sem.at[step, 1],
                device_id=(zone, rank - 1), device_id_type=MESH,
            ),
        )

    def start_halos(step):
        up, down = halos(step)

        @pl.when(rank < RANKS - 1)
        def _():
            up.start()

        @pl.when(rank > 0)
        def _():
            down.start()

    def wait_halos(step):
        up, down = halos(step)

        @pl.when(rank > 0)
        def _():
            up.wait_recv()

        @pl.when(rank == 0)
        def _():
            halo_in[step, 0] = jnp.zeros((B, LANES), F32)

        @pl.when(rank < RANKS - 1)
        def _():
            down.wait_recv()

        @pl.when(rank == RANKS - 1)
        def _():
            halo_in[step, 1] = jnp.zeros((B, LANES), F32)

        @pl.when(rank < RANKS - 1)
        def _():
            up.wait_send()

        @pl.when(rank > 0)
        def _():
            down.wait_send()

    def rows_from(tiles):
        tiles = [
            jnp.where(sub < 4, one, two) + pltpu.roll(jnp.where(sub < 4, two, one), 4, 0)
            for one, two in zip(tiles[:4], tiles[4:])
        ]
        for shift in (2, 1):
            half = len(tiles) // 2
            tiles = [
                jnp.where(sub % (2 * shift) < shift, one + pltpu.roll(one, 8 - shift, 0), two + pltpu.roll(two, shift, 0))
                for one, two in zip(tiles[:half], tiles[half:])
            ]
        return tiles[0]

    def apply_precond(step):
        def rows_of(block, _):
            first = pl.multiple_of(block * 8, 8)
            for c in range(2):
                half = slice(c * LANES, c * LANES + LANES)
                vector = [near[0, t * 8 : t * 8 + 8, half] for t in range(TILES)]
                halo_out[step, c, pl.ds(first, 8), :] = rows_from([
                    add_up(precond[first + i, t * 8 : t * 8 + 8, half] * vector[t] for t in range(TILES)) for i in range(8)
                ])
            return 0

        lax.fori_loop(0, TILES, rows_of, 0, unroll=TILES)

    def expand_counts(c):
        tile = jnp.broadcast_to(counts[...], (8, LANES))
        return gather_lanes(tile, c * 32 + lane // CAP)

    def gather_sending(step, c):
        at = jnp.broadcast_to(rows[pl.ds(c, 1), :], (8, LANES))
        live = jnp.where(lane % CAP < expand_counts(c), 1.0, 0.0)
        low, at = at < LANES, at % LANES
        for t in range(TILES):
            first = gather_lanes(halo_out[step, 0, t * 8 : t * 8 + 8, :], at)
            second = gather_lanes(halo_out[step, 1, t * 8 : t * 8 + 8, :], at)
            sending[c, t * 8 : t * 8 + 8, :] = jnp.where(low, first, second) * live

    def couple(pair_of):
        def step_of(i, acc):
            row = pl.multiple_of(i * B, 8)
            added = []
            for c in pair_of:
                factor = jnp.broadcast_to(sending[c, pl.ds(i, 1), :], (8, LANES))
                added += [stash[c, pl.ds(row + t * 8, 8), :] * factor for t in range(TILES)]
            return tuple(old + new for old, new in zip(acc, added))

        zero = jnp.zeros((8, LANES), F32)
        sums = lax.fori_loop(0, B, step_of, (zero,) * (2 * TILES), unroll=B)
        return sums[:TILES], sums[TILES:]

    def pack(step, p, couplings, scalars):
        zero = jnp.zeros((8, LANES), F32)
        tiles = []
        for h in range(2):
            for t in range(TILES):
                first = gather_lanes(couplings[0][t], pair + h)
                second = gather_lanes(couplings[1][t], pair + h)
                tiles.append(jnp.where(left, first, second))
            first = gather_lanes(jnp.broadcast_to(cols[pl.ds(2 * p, 1), :], (8, LANES)), pair + h)
            second = gather_lanes(jnp.broadcast_to(cols[pl.ds(2 * p + 1, 1), :], (8, LANES)), pair + h)
            extra = jnp.where(sub == 0, jnp.where(left, first, second).astype(F32), 0.0)
            for place_of, scalar in enumerate(scalars):
                extra = jnp.where(sub == 1 + place_of, scalar, extra)
            tiles += [extra, zero, zero]
        turned = jnp.concatenate(tiles, axis=0).T
        for d in range(64):
            send[step, 64 * p + d] = turned[2 * d : 2 * d + 2, :]

    def message(step, kind, offset):
        z, r = (zone + ahead[kind]) % 4, rank_at(offset)
        spot = offset[0] * 8 + offset[1] * 2 + offset[2]
        return pltpu.make_async_remote_copy(
            src_ref=send.at[step, z * RANKS + r], dst_ref=arrived.at[step, ahead[kind] * RANKS + spot],
            send_sem=send_sem.at[step], recv_sem=recv_sem.at[step],
            device_id=(z, r), device_id_type=MESH,
        )

    def own(step):
        return pltpu.make_async_copy(send.at[step, me], arrived.at[step, 0], own_sem.at[step])

    def all_arrived(step):
        others = arrived.at[step, pl.ds(1, DEVICES - 1)]
        pltpu.make_async_copy(others, others, recv_sem.at[step]).wait()
        own(step).wait()

    def prepare(step, k, scalars):
        pair_of = chunks[2 * k : 2 * k + 2]
        for j, c in enumerate(pair_of):
            if step == 0:
                load_stash[2 * k + j].wait()
            gather_sending(step, c)
        pack(step, pairs[k], couple(pair_of), scalars)

    def first_out(other):
        return other[0] > 0 and other[0] + plane_hops(other[1]) >= 4

    def post(step, first):
        for other in KINDS:
            if first_out(other) == first:
                message(step, *other).start()

    def apply_local(step):
        for t in range(TILES):
            tile = slice(t * 8, t * 8 + 8)
            zero_tile = halo_out[step, 0, tile, :]
            one_tile = halo_out[step, 1, tile, :]
            rim_tile = jnp.where(left, halo_in[step, 1, tile, :], halo_in[step, 0, tile, :])
            near[0, tile, :LANES] = zero_tile
            near[0, tile, LANES:] = one_tile
            for f in range(6):
                for c in range(2):
                    at = jnp.broadcast_to(nbrs[f : f + 1, c * LANES : c * LANES + LANES], (8, LANES))
                    index = (at + 64) % LANES
                    found = jnp.where(
                        (at >= 64) & (at < 192), gather_lanes(zero_tile, index),
                        jnp.where((at >= 192) & (at < 320), gather_lanes(one_tile, index), gather_lanes(rim_tile, index)),
                    )
                    near[1 + f, tile, c * LANES : c * LANES + LANES] = found
        if step == 0:
            load_diag.wait()
            load_face.wait()

        def rows_of(block, _):
            first = pl.multiple_of(block * 8, 8)
            for c in range(2):
                half = slice(c * LANES, c * LANES + LANES)
                sums = [None] * 8
                for b in range(7):
                    vector = [near[b, t * 8 : t * 8 + 8, half] for t in range(TILES)]
                    for i in range(8):
                        term = add_up(blocks[b, first + i, t * 8 : t * 8 + 8, half] * vector[t] for t in range(TILES))
                        sums[i] = term if b == 0 else sums[i] + term
                image[pl.ds(first, 8), half] = rows_from(sums)
            return 0

        lax.fori_loop(0, TILES, rows_of, 0)

    def received(step):
        return jnp.concatenate([arrived[step, k] for k in range(DEVICES)], axis=0)

    def sums_of(table):
        tile = add_up(table[8 * k : 8 * k + 8, :] for k in range(2 * DEVICES // 8))
        return jnp.sum(tile, axis=0, keepdims=True) * 0.5

    def scattered(table):
        turned = table.T
        halves = []
        for h in range(2):
            rest = turned[64 * h : 64 * h + 48, :]
            parts = []
            for _ in range(3):
                part = rest.astype(jnp.bfloat16)
                parts.append(part)
                rest = rest - part.astype(F32)
            halves.append(jnp.concatenate(parts, axis=0))
        product = jnp.dot(jnp.concatenate(halves, axis=1), onehot[...], preferred_element_type=F32)
        return product[:B] + product[48 : 48 + B] + product[96 : 96 + B]

    small[0].wait()
    near[0] = rhs[...] * DOWN
    square = total(rhs[...] * rhs[...])
    load_precond.wait()
    apply_precond(0)
    small[1].wait()
    small[2].wait()
    small[3].wait()
    small[4].wait()
    for k in range(2):
        prepare(0, k, (square,))
    pl.semaphore_wait(barrier, DEVICES - 1)
    post(0, True)
    start_halos(0)
    post(0, False)
    own(0).start()
    wait_halos(0)
    apply_local(0)
    all_arrived(0)
    table = received(0)
    element = lax.broadcasted_iota(jnp.int32, (256, 256), 1).astype(F32)
    for h in range(2):
        column = table[:, 64 * h + B : 64 * h + B + 1]
        onehot[256 * h : 256 * h + 256, :] = jnp.where(element == column, 1.0, 0.0).astype(jnp.bfloat16)
    sums = sums_of(table)
    square = sums[:, B + 1 : B + 2]
    beta = jnp.sqrt(square + EPS)
    shrunk = 1.0 / beta
    basis0 = rhs[...] * shrunk
    factor = UP * shrunk
    work0 = (image[...] + scattered(table)) * factor
    search0[:, :LANES] = halo_out[0, 0] * factor
    search0[:, LANES:] = halo_out[0, 1] * factor

    near[0] = work0
    apply_precond(1)
    scalars = (total(work0 * basis0), total(work0 * work0))
    prepare(1, 0, scalars)
    post(1, True)
    start_halos(1)
    prepare(1, 1, scalars)
    post(1, False)
    own(1).start()
    wait_halos(1)
    apply_local(1)
    all_arrived(1)
    table = received(1)
    sums = sums_of(table)
    h00 = sums[:, B + 1 : B + 2]
    shrink = 1.0 / jnp.sqrt(sums[:, B + 2 : B + 3] + EPS)
    unit = square / (square + EPS)
    work1 = work0 - h00 * basis0
    second = (image[...] + scattered(table) - h00 * work0) * shrink

    values = (
        total(work1 * work1), total(work1 * basis0), total(second * basis0), total(second * work1), total(second * second)
    )
    row_lane = lax.broadcasted_iota(jnp.int32, (1, LANES), 1)
    mine = jnp.zeros((1, LANES), F32)
    for place_of, value in enumerate(values):
        mine = jnp.where(row_lane == place_of, value, mine)
    dots[...] = mine
    dots_in[0] = mine

    def tell(other):
        dz, (dy, dx, dc) = other
        return pltpu.make_async_remote_copy(
            src_ref=dots, dst_ref=dots_in.at[dz * RANKS + dy * 8 + dx * 2 + dc],
            send_sem=send_sem.at[2], recv_sem=recv_sem.at[2],
            device_id=place(other), device_id_type=MESH,
        )

    for other in OTHERS:
        tell(other).start()
    others = dots_in.at[pl.ds(1, DEVICES - 1)]
    pltpu.make_async_copy(others, others, recv_sem.at[2]).wait()
    sums = add_up(dots_in[k] for k in range(DEVICES))
    n1, cross, a, b, d = (sums[:, k : k + 1] for k in range(5))
    n1_eps = n1 + EPS
    across = b - a * cross
    along = across / n1_eps
    left_over = d - 2.0 * a * a + unit * a * a - 2.0 * along * b + along * along * n1 + 2.0 * a * along * cross
    n00 = h00 * h00 + n1_eps
    mixed = h00 * a + across
    lower = mixed / n00
    corner = a * a + along * across + (jnp.maximum(left_over, 0.0) + EPS * n1_eps * shrink * shrink)
    y1 = beta * (a - lower * h00) / (corner - lower * mixed)
    c0 = (beta * h00 - mixed * y1) / n00
    y1_small = y1 * shrink
    own_part = c0 - y1_small * h00
    for c in range(2):
        half = slice(c * LANES, c * LANES + LANES)
        out_ref[0, :, half] = own_part * search0[:, half] + y1_small * halo_out[1, c]
    out_ref[1] = rhs[...] - c0 * work0 - y1 * second

    for step in range(2):
        others = arrived.at[step, pl.ds(1, DEVICES - 1)]
        pltpu.make_async_copy(others, others, send_sem.at[step]).wait()
    others = dots_in.at[pl.ds(1, DEVICES - 1)]
    pltpu.make_async_copy(others, others, send_sem.at[2]).wait()


def per_device(rhs, diag, precond, face, nbrs, stash, rows, cols, counts):
    arrays = (
        rhs, diag, precond, face, nbrs, stash, rows.reshape(4, LANES), cols.reshape(4, LANES), counts.reshape(1, LANES)
    )
    anywhere = pl.BlockSpec(memory_space=pl.ANY)
    out = pl.pallas_call(
        kernel,
        out_shape=jax.ShapeDtypeStruct((2, B, 256), F32),
        in_specs=[anywhere] * 9,
        out_specs=pl.BlockSpec(memory_space=pltpu.VMEM),
        scratch_shapes=[
            pltpu.VMEM((B, 256), F32),
            pltpu.VMEM((B, B, 256), F32),
            pltpu.VMEM((7, B, B, 256), F32),
            pltpu.VMEM((4, B * B, LANES), F32),
            pltpu.VMEM((6, 256), jnp.int32),
            pltpu.VMEM((4, LANES), jnp.int32),
            pltpu.VMEM((4, LANES), jnp.int32),
            pltpu.VMEM((1, LANES), jnp.int32),
            pltpu.VMEM((7, B, 256), F32),
            pltpu.VMEM((2, 2, B, LANES), F32),
            pltpu.VMEM((2, 2, B, LANES), F32),
            pltpu.VMEM((B, 256), F32),
            pltpu.VMEM((B, 256), F32),
            pltpu.VMEM((4, B, LANES), F32),
            pltpu.VMEM((2, DEVICES, 2, LANES), F32),
            pltpu.VMEM((2, DEVICES, 2, LANES), F32),
            pltpu.VMEM((512, 256), jnp.bfloat16),
            pltpu.VMEM((1, LANES), F32),
            pltpu.VMEM((DEVICES, 1, LANES), F32),
            pltpu.SemaphoreType.DMA((12,)),
            pltpu.SemaphoreType.DMA((2,)),
            pltpu.SemaphoreType.DMA((3,)),
            pltpu.SemaphoreType.DMA((3,)),
            pltpu.SemaphoreType.DMA((2, 2)),
            pltpu.SemaphoreType.DMA((2, 2)),
        ],
        compiler_params=pltpu.CompilerParams(
            collective_id=0, has_side_effects=True, vmem_limit_bytes=48 * 2**20
        ),
        name="gmres",
    )(*(pltpu.with_memory_space_constraint(array, pltpu.HBM) for array in arrays))
    return out[0], out[1]


def solution(mesh):
    spread = ("zone", "rank")
    return jax.shard_map(
        per_device,
        mesh=mesh,
        in_specs=(
            P(None, spread),
            P(None, None, spread),
            P(None, None, spread),
            P(None, None, None, spread),
            P(None, spread),
            P(None, spread),
            P(spread),
            P(spread),
            P(spread),
        ),
        out_specs=(P(None, spread), P(None, spread)),
        check_vma=False,
    )
```

```python
import jax
import jax.numpy as jnp
from jax import lax
from jax.experimental import pallas as pl
from jax.experimental.pallas import tpu as pltpu
from jax.sharding import PartitionSpec as P

B = 40
TILES = B // 8
LANES = 128
ZONES, RANKS = 4, 32
DEVICES = ZONES * RANKS
CAP = 4
EPS = 1e-6
DOWN = 2.0**-40
UP = 2.0**40
MESH = pl.DeviceIdType.MESH
F32 = jnp.float32

HOPS = (0, 1, 2, 1)
PLANE = [(dy, dx, dc) for dy in range(4) for dx in range(4) for dc in range(2)]


def plane_hops(offset):
    return HOPS[offset[0]] + HOPS[offset[1]]


OTHERS = sorted(
    ((dz, offset) for dz in range(4) for offset in PLANE if dz or any(offset)),
    key=lambda other: -(HOPS[other[0]] + plane_hops(other[1])),
)
KINDS = sorted(
    ((kind, offset) for kind in (2, 1, -1, 0) for offset in PLANE if kind or any(offset)),
    key=lambda other: -(abs(other[0]) + plane_hops(other[1])),
)


def gather_lanes(tile, index):
    return jnp.take_along_axis(tile, index, axis=1)


def add_up(terms):
    terms = list(terms)
    while len(terms) > 1:
        terms = [terms[k] + terms[k + 1] if k + 1 < len(terms) else terms[k] for k in range(0, len(terms), 2)]
    return terms[0]


def total(value):
    return jnp.sum(jnp.sum(value, axis=0, keepdims=True), axis=1, keepdims=True)


def kernel(
    rhs_hbm, diag_hbm, precond_hbm, face_hbm, nbrs_hbm, stash_hbm, rows_hbm, cols_hbm, counts_hbm,
    out_ref,
    rhs, precond, blocks, stash, nbrs, rows, cols, counts,
    near, halo_out, halo_in, search0, image, sending,
    send, arrived, onehot, dots, dots_in,
    load_sem, own_sem, send_sem, recv_sem, halo_send_sem, halo_recv_sem,
):
    zone, rank = lax.axis_index("zone"), lax.axis_index("rank")
    y, x, core = rank // 8, (rank // 2) % 4, rank % 2
    me = zone * RANKS + rank
    zs = [(zone + d) % 4 for d in range(4)]
    ys = [((y + d) % 4) * 8 for d in range(4)]
    xs = [((x + d) % 4) * 2 for d in range(4)]
    cs = [(core + d) % 2 for d in range(2)]
    yxs = [[ys[a] + xs[b] for b in range(4)] for a in range(4)]

    def rank_at(offset):
        dy, dx, dc = offset
        return yxs[dy][dx] + cs[dc]

    def place(other):
        return zs[other[0]], rank_at(other[1])

    mate = 3 - 2 * (zone % 2)
    ahead = {2: 2, 1: mate, -1: 4 - mate, 0: 0}
    far_pair = ((zone + 2) % 4) // 2
    pairs = (far_pair, 1 - far_pair)
    chunks = tuple(2 * p + k for p in pairs for k in range(2))

    barrier = pltpu.get_barrier_semaphore()

    def greet(others):
        for other in others:
            pl.semaphore_signal(barrier, inc=1, device_id=place(other), device_id_type=MESH)

    greet(OTHERS)

    small = [
        pltpu.make_async_copy(rhs_hbm, rhs, load_sem.at[0]),
        pltpu.make_async_copy(rows_hbm, rows, load_sem.at[1]),
        pltpu.make_async_copy(counts_hbm, counts, load_sem.at[2]),
        pltpu.make_async_copy(cols_hbm, cols, load_sem.at[3]),
        pltpu.make_async_copy(nbrs_hbm, nbrs, load_sem.at[4]),
    ]
    load_precond = pltpu.make_async_copy(precond_hbm, precond, load_sem.at[5])
    load_stash = [
        pltpu.make_async_copy(
            stash_hbm.at[:, pl.ds(pl.multiple_of(c * LANES, LANES), LANES)], stash.at[c], load_sem.at[6 + k]
        )
        for k, c in enumerate(chunks)
    ]
    load_diag = pltpu.make_async_copy(diag_hbm, blocks.at[0], load_sem.at[10])
    load_face = pltpu.make_async_copy(face_hbm, blocks.at[pl.ds(1, 6)], load_sem.at[11])
    for load in [*small, load_precond, *load_stash, load_diag, load_face]:
        load.start()

    lane = lax.broadcasted_iota(jnp.int32, (8, LANES), 1)
    sub = lax.broadcasted_iota(jnp.int32, (8, LANES), 0)
    left = lane < LANES // 2
    pair = 2 * (lane % (LANES // 2))

    def halos(step):
        return (
            pltpu.make_async_remote_copy(
                src_ref=halo_out.at[step, 1], dst_ref=halo_in.at[step, 0],
                send_sem=halo_send_sem.at[step, 0], recv_sem=halo_recv_sem.at[step, 0],
                device_id=(zone, rank + 1), device_id_type=MESH,
            ),
            pltpu.make_async_remote_copy(
                src_ref=halo_out.at[step, 0], dst_ref=halo_in.at[step, 1],
                send_sem=halo_send_sem.at[step, 1], recv_sem=halo_recv_sem.at[step, 1],
                device_id=(zone, rank - 1), device_id_type=MESH,
            ),
        )

    def start_halos(step):
        up, down = halos(step)

        @pl.when(rank < RANKS - 1)
        def _():
            up.start()

        @pl.when(rank > 0)
        def _():
            down.start()

    def wait_halos(step):
        up, down = halos(step)

        @pl.when(rank > 0)
        def _():
            up.wait_recv()

        @pl.when(rank == 0)
        def _():
            halo_in[step, 0] = jnp.zeros((B, LANES), F32)

        @pl.when(rank < RANKS - 1)
        def _():
            down.wait_recv()

        @pl.when(rank == RANKS - 1)
        def _():
            halo_in[step, 1] = jnp.zeros((B, LANES), F32)

        @pl.when(rank < RANKS - 1)
        def _():
            up.wait_send()

        @pl.when(rank > 0)
        def _():
            down.wait_send()

    def rows_from(tiles):
        tiles = [
            jnp.where(sub < 4, one, two) + pltpu.roll(jnp.where(sub < 4, two, one), 4, 0)
            for one, two in zip(tiles[:4], tiles[4:])
        ]
        for shift in (2, 1):
            half = len(tiles) // 2
            tiles = [
                jnp.where(sub % (2 * shift) < shift, one + pltpu.roll(one, 8 - shift, 0), two + pltpu.roll(two, shift, 0))
                for one, two in zip(tiles[:half], tiles[half:])
            ]
        return tiles[0]

    def apply_precond(step):
        def rows_of(block, _):
            first = pl.multiple_of(block * 8, 8)
            for c in range(2):
                half = slice(c * LANES, c * LANES + LANES)
                vector = [near[0, t * 8 : t * 8 + 8, half] for t in range(TILES)]
                halo_out[step, c, pl.ds(first, 8), :] = rows_from([
                    add_up(precond[first + i, t * 8 : t * 8 + 8, half] * vector[t] for t in range(TILES)) for i in range(8)
                ])
            return 0

        lax.fori_loop(0, TILES, rows_of, 0, unroll=TILES)

    def expand_counts(c):
        tile = jnp.broadcast_to(counts[...], (8, LANES))
        return gather_lanes(tile, c * 32 + lane // CAP)

    def gather_sending(step, c):
        at = jnp.broadcast_to(rows[pl.ds(c, 1), :], (8, LANES))
        live = jnp.where(lane % CAP < expand_counts(c), 1.0, 0.0)
        low, at = at < LANES, at % LANES
        for t in range(TILES):
            first = gather_lanes(halo_out[step, 0, t * 8 : t * 8 + 8, :], at)
            second = gather_lanes(halo_out[step, 1, t * 8 : t * 8 + 8, :], at)
            sending[c, t * 8 : t * 8 + 8, :] = jnp.where(low, first, second) * live

    def couple(pair_of):
        def step_of(i, acc):
            row = pl.multiple_of(i * B, 8)
            added = []
            for c in pair_of:
                factor = jnp.broadcast_to(sending[c, pl.ds(i, 1), :], (8, LANES))
                added += [stash[c, pl.ds(row + t * 8, 8), :] * factor for t in range(TILES)]
            return tuple(old + new for old, new in zip(acc, added))

        zero = jnp.zeros((8, LANES), F32)
        sums = lax.fori_loop(0, B, step_of, (zero,) * (2 * TILES), unroll=B)
        return sums[:TILES], sums[TILES:]

    def pack(step, p, couplings, scalars):
        zero = jnp.zeros((8, LANES), F32)
        tiles = []
        for h in range(2):
            for t in range(TILES):
                first = gather_lanes(couplings[0][t], pair + h)
                second = gather_lanes(couplings[1][t], pair + h)
                tiles.append(jnp.where(left, first, second))
            first = gather_lanes(jnp.broadcast_to(cols[pl.ds(2 * p, 1), :], (8, LANES)), pair + h)
            second = gather_lanes(jnp.broadcast_to(cols[pl.ds(2 * p + 1, 1), :], (8, LANES)), pair + h)
            extra = jnp.where(sub == 0, jnp.where(left, first, second).astype(F32), 0.0)
            for place_of, scalar in enumerate(scalars):
                extra = jnp.where(sub == 1 + place_of, scalar, extra)
            tiles += [extra, zero, zero]
        turned = jnp.concatenate(tiles, axis=0).T
        for d in range(64):
            send[step, 64 * p + d] = turned[2 * d : 2 * d + 2, :]

    def message(step, kind, offset):
        z, r = (zone + ahead[kind]) % 4, rank_at(offset)
        spot = offset[0] * 8 + offset[1] * 2 + offset[2]
        return pltpu.make_async_remote_copy(
            src_ref=send.at[step, z * RANKS + r], dst_ref=arrived.at[step, ahead[kind] * RANKS + spot],
            send_sem=send_sem.at[step], recv_sem=recv_sem.at[step],
            device_id=(z, r), device_id_type=MESH,
        )

    def own(step):
        return pltpu.make_async_copy(send.at[step, me], arrived.at[step, 0], own_sem.at[step])

    def all_arrived(step):
        others = arrived.at[step, pl.ds(1, DEVICES - 1)]
        pltpu.make_async_copy(others, others, recv_sem.at[step]).wait()
        own(step).wait()

    def prepare(step, k, scalars):
        pair_of = chunks[2 * k : 2 * k + 2]
        for j, c in enumerate(pair_of):
            if step == 0:
                load_stash[2 * k + j].wait()
            gather_sending(step, c)
        pack(step, pairs[k], couple(pair_of), scalars)

    def first_out(other):
        return other[0] > 0

    def post(step, first):
        for other in KINDS:
            if first_out(other) == first:
                message(step, *other).start()

    def apply_local(step):
        for t in range(TILES):
            tile = slice(t * 8, t * 8 + 8)
            zero_tile = halo_out[step, 0, tile, :]
            one_tile = halo_out[step, 1, tile, :]
            rim_tile = jnp.where(left, halo_in[step, 1, tile, :], halo_in[step, 0, tile, :])
            near[0, tile, :LANES] = zero_tile
            near[0, tile, LANES:] = one_tile
            for f in range(6):
                for c in range(2):
                    at = jnp.broadcast_to(nbrs[f : f + 1, c * LANES : c * LANES + LANES], (8, LANES))
                    index = (at + 64) % LANES
                    found = jnp.where(
                        (at >= 64) & (at < 192), gather_lanes(zero_tile, index),
                        jnp.where((at >= 192) & (at < 320), gather_lanes(one_tile, index), gather_lanes(rim_tile, index)),
                    )
                    near[1 + f, tile, c * LANES : c * LANES + LANES] = found
        if step == 0:
            load_diag.wait()
            load_face.wait()

        def rows_of(block, _):
            first = pl.multiple_of(block * 8, 8)
            for c in range(2):
                half = slice(c * LANES, c * LANES + LANES)
                sums = [None] * 8
                for b in range(7):
                    vector = [near[b, t * 8 : t * 8 + 8, half] for t in range(TILES)]
                    for i in range(8):
                        term = add_up(blocks[b, first + i, t * 8 : t * 8 + 8, half] * vector[t] for t in range(TILES))
                        sums[i] = term if b == 0 else sums[i] + term
                image[pl.ds(first, 8), half] = rows_from(sums)
            return 0

        lax.fori_loop(0, TILES, rows_of, 0)

    def received(step):
        return jnp.concatenate([arrived[step, k] for k in range(DEVICES)], axis=0)

    def sums_of(table):
        tile = add_up(table[8 * k : 8 * k + 8, :] for k in range(2 * DEVICES // 8))
        return jnp.sum(tile, axis=0, keepdims=True) * 0.5

    def scattered(table):
        turned = table.T
        halves = []
        for h in range(2):
            rest = turned[64 * h : 64 * h + 48, :]
            parts = []
            for _ in range(3):
                part = rest.astype(jnp.bfloat16)
                parts.append(part)
                rest = rest - part.astype(F32)
            halves.append(jnp.concatenate(parts, axis=0))
        product = jnp.dot(jnp.concatenate(halves, axis=1), onehot[...], preferred_element_type=F32)
        return product[:B] + product[48 : 48 + B] + product[96 : 96 + B]

    small[0].wait()
    near[0] = rhs[...] * DOWN
    square = total(rhs[...] * rhs[...])
    load_precond.wait()
    apply_precond(0)
    small[1].wait()
    small[2].wait()
    small[3].wait()
    small[4].wait()
    for k in range(2):
        prepare(0, k, (square,))
    pl.semaphore_wait(barrier, DEVICES - 1)
    post(0, True)
    start_halos(0)
    post(0, False)
    own(0).start()
    wait_halos(0)
    apply_local(0)
    all_arrived(0)
    table = received(0)
    element = lax.broadcasted_iota(jnp.int32, (256, 256), 1).astype(F32)
    for h in range(2):
        column = table[:, 64 * h + B : 64 * h + B + 1]
        onehot[256 * h : 256 * h + 256, :] = jnp.where(element == column, 1.0, 0.0).astype(jnp.bfloat16)
    sums = sums_of(table)
    square = sums[:, B + 1 : B + 2]
    beta = jnp.sqrt(square + EPS)
    shrunk = 1.0 / beta
    basis0 = rhs[...] * shrunk
    factor = UP * shrunk
    work0 = (image[...] + scattered(table)) * factor
    search0[:, :LANES] = halo_out[0, 0] * factor
    search0[:, LANES:] = halo_out[0, 1] * factor

    near[0] = work0
    apply_precond(1)
    scalars = (total(work0 * basis0), total(work0 * work0))
    prepare(1, 0, scalars)
    post(1, True)
    start_halos(1)
    prepare(1, 1, scalars)
    post(1, False)
    own(1).start()
    wait_halos(1)
    apply_local(1)
    all_arrived(1)
    table = received(1)
    sums = sums_of(table)
    h00 = sums[:, B + 1 : B + 2]
    shrink = 1.0 / jnp.sqrt(sums[:, B + 2 : B + 3] + EPS)
    unit = square / (square + EPS)
    work1 = work0 - h00 * basis0
    second = (image[...] + scattered(table) - h00 * work0) * shrink

    values = (
        total(work1 * work1), total(work1 * basis0), total(second * basis0), total(second * work1), total(second * second)
    )
    row_lane = lax.broadcasted_iota(jnp.int32, (1, LANES), 1)
    mine = jnp.zeros((1, LANES), F32)
    for place_of, value in enumerate(values):
        mine = jnp.where(row_lane == place_of, value, mine)
    dots[...] = mine
    dots_in[0] = mine

    def tell(other):
        dz, (dy, dx, dc) = other
        return pltpu.make_async_remote_copy(
            src_ref=dots, dst_ref=dots_in.at[dz * RANKS + dy * 8 + dx * 2 + dc],
            send_sem=send_sem.at[2], recv_sem=recv_sem.at[2],
            device_id=place(other), device_id_type=MESH,
        )

    for other in OTHERS:
        tell(other).start()
    others = dots_in.at[pl.ds(1, DEVICES - 1)]
    pltpu.make_async_copy(others, others, recv_sem.at[2]).wait()
    sums = add_up(dots_in[k] for k in range(DEVICES))
    n1, cross, a, b, d = (sums[:, k : k + 1] for k in range(5))
    n1_eps = n1 + EPS
    across = b - a * cross
    along = across / n1_eps
    left_over = d - 2.0 * a * a + unit * a * a - 2.0 * along * b + along * along * n1 + 2.0 * a * along * cross
    n00 = h00 * h00 + n1_eps
    mixed = h00 * a + across
    lower = mixed / n00
    corner = a * a + along * across + (jnp.maximum(left_over, 0.0) + EPS * n1_eps * shrink * shrink)
    y1 = beta * (a - lower * h00) / (corner - lower * mixed)
    c0 = (beta * h00 - mixed * y1) / n00
    y1_small = y1 * shrink
    own_part = c0 - y1_small * h00
    for c in range(2):
        half = slice(c * LANES, c * LANES + LANES)
        out_ref[0, :, half] = own_part * search0[:, half] + y1_small * halo_out[1, c]
    out_ref[1] = rhs[...] - c0 * work0 - y1 * second

    for step in range(2):
        others = arrived.at[step, pl.ds(1, DEVICES - 1)]
        pltpu.make_async_copy(others, others, send_sem.at[step]).wait()
    others = dots_in.at[pl.ds(1, DEVICES - 1)]
    pltpu.make_async_copy(others, others, send_sem.at[2]).wait()


def per_device(rhs, diag, precond, face, nbrs, stash, rows, cols, counts):
    arrays = (
        rhs, diag, precond, face, nbrs, stash, rows.reshape(4, LANES), cols.reshape(4, LANES), counts.reshape(1, LANES)
    )
    anywhere = pl.BlockSpec(memory_space=pl.ANY)
    out = pl.pallas_call(
        kernel,
        out_shape=jax.ShapeDtypeStruct((2, B, 256), F32),
        in_specs=[anywhere] * 9,
        out_specs=pl.BlockSpec(memory_space=pltpu.VMEM),
        scratch_shapes=[
            pltpu.VMEM((B, 256), F32),
            pltpu.VMEM((B, B, 256), F32),
            pltpu.VMEM((7, B, B, 256), F32),
            pltpu.VMEM((4, B * B, LANES), F32),
            pltpu.VMEM((6, 256), jnp.int32),
            pltpu.VMEM((4, LANES), jnp.int32),
            pltpu.VMEM((4, LANES), jnp.int32),
            pltpu.VMEM((1, LANES), jnp.int32),
            pltpu.VMEM((7, B, 256), F32),
            pltpu.VMEM((2, 2, B, LANES), F32),
            pltpu.VMEM((2, 2, B, LANES), F32),
            pltpu.VMEM((B, 256), F32),
            pltpu.VMEM((B, 256), F32),
            pltpu.VMEM((4, B, LANES), F32),
            pltpu.VMEM((2, DEVICES, 2, LANES), F32),
            pltpu.VMEM((2, DEVICES, 2, LANES), F32),
            pltpu.VMEM((512, 256), jnp.bfloat16),
            pltpu.VMEM((1, LANES), F32),
            pltpu.VMEM((DEVICES, 1, LANES), F32),
            pltpu.SemaphoreType.DMA((12,)),
            pltpu.SemaphoreType.DMA((2,)),
            pltpu.SemaphoreType.DMA((3,)),
            pltpu.SemaphoreType.DMA((3,)),
            pltpu.SemaphoreType.DMA((2, 2)),
            pltpu.SemaphoreType.DMA((2, 2)),
        ],
        compiler_params=pltpu.CompilerParams(
            collective_id=0, has_side_effects=True, vmem_limit_bytes=48 * 2**20
        ),
        name="gmres",
    )(*(pltpu.with_memory_space_constraint(array, pltpu.HBM) for array in arrays))
    return out[0], out[1]


def solution(mesh):
    spread = ("zone", "rank")
    return jax.shard_map(
        per_device,
        mesh=mesh,
        in_specs=(
            P(None, spread),
            P(None, None, spread),
            P(None, None, spread),
            P(None, None, None, spread),
            P(None, spread),
            P(None, spread),
            P(spread),
            P(spread),
            P(spread),
        ),
        out_specs=(P(None, spread), P(None, spread)),
        check_vma=False,
    )
```

```python
import jax
import jax.numpy as jnp
from jax import lax
from jax.experimental import pallas as pl
from jax.experimental.pallas import tpu as pltpu
from jax.sharding import PartitionSpec as P

B = 40
TILES = B // 8
RIM_TILES = (TILES + 1) // 2
LANES = 128
ZONES, RANKS = 4, 32
DEVICES = ZONES * RANKS
CAP = 4
EPS = 1e-6
DOWN = 2.0**-40
UP = 2.0**40
MESH = pl.DeviceIdType.MESH
F32 = jnp.float32

HOPS = (0, 1, 2, 1)
PLANE = [(dy, dx, dc) for dy in range(4) for dx in range(4) for dc in range(2)]


def plane_hops(offset):
    return HOPS[offset[0]] + HOPS[offset[1]]


OTHERS = sorted(
    ((dz, offset) for dz in range(4) for offset in PLANE if dz or any(offset)),
    key=lambda other: -(HOPS[other[0]] + plane_hops(other[1])),
)
KINDS = sorted(
    ((kind, offset) for kind in (2, 1, -1, 0) for offset in PLANE if kind or any(offset)),
    key=lambda other: -(abs(other[0]) + plane_hops(other[1])),
)


def gather_lanes(tile, index):
    return jnp.take_along_axis(tile, index, axis=1)


def half_turn(tile):
    return pltpu.roll(tile, LANES // 2, 1)


def add_up(terms):
    terms = list(terms)
    while len(terms) > 1:
        terms = [terms[k] + terms[k + 1] if k + 1 < len(terms) else terms[k] for k in range(0, len(terms), 2)]
    return terms[0]


def total(value):
    return jnp.sum(jnp.sum(value, axis=0, keepdims=True), axis=1, keepdims=True)


def kernel(
    rhs_hbm, diag_hbm, precond_hbm, face_hbm, nbrs_hbm, stash_hbm, rows_hbm, cols_hbm, counts_hbm,
    out_ref,
    rhs, precond, blocks, stash, nbrs, rows, cols, counts,
    near, search, rim_out, rim_in, search0, image, sending,
    send, arrived, onehot, dots, dots_in,
    load_sem, own_sem, send_sem, recv_sem, halo_send_sem, halo_recv_sem,
):
    zone, rank = lax.axis_index("zone"), lax.axis_index("rank")
    y, x, core = rank // 8, (rank // 2) % 4, rank % 2
    me = zone * RANKS + rank
    zs = [(zone + d) % 4 for d in range(4)]
    ys = [((y + d) % 4) * 8 for d in range(4)]
    xs = [((x + d) % 4) * 2 for d in range(4)]
    cs = [(core + d) % 2 for d in range(2)]
    yxs = [[ys[a] + xs[b] for b in range(4)] for a in range(4)]

    def rank_at(offset):
        dy, dx, dc = offset
        return yxs[dy][dx] + cs[dc]

    def place(other):
        return zs[other[0]], rank_at(other[1])

    mate = 3 - 2 * (zone % 2)
    ahead = {2: 2, 1: mate, -1: 4 - mate, 0: 0}
    far_pair = ((zone + 2) % 4) // 2
    pairs = (far_pair, 1 - far_pair)
    chunks = tuple(2 * p + k for p in pairs for k in range(2))

    barrier = pltpu.get_barrier_semaphore()

    def greet(others):
        for other in others:
            pl.semaphore_signal(barrier, inc=1, device_id=place(other), device_id_type=MESH)

    greet(OTHERS)

    small = [
        pltpu.make_async_copy(rhs_hbm, rhs, load_sem.at[0]),
        pltpu.make_async_copy(rows_hbm, rows, load_sem.at[1]),
        pltpu.make_async_copy(counts_hbm, counts, load_sem.at[2]),
        pltpu.make_async_copy(cols_hbm, cols, load_sem.at[3]),
        pltpu.make_async_copy(nbrs_hbm, nbrs, load_sem.at[4]),
    ]
    load_precond = pltpu.make_async_copy(precond_hbm, precond, load_sem.at[5])
    load_stash = [
        pltpu.make_async_copy(
            stash_hbm.at[:, pl.ds(pl.multiple_of(c * LANES, LANES), LANES)], stash.at[c], load_sem.at[6 + k]
        )
        for k, c in enumerate(chunks)
    ]
    load_diag = pltpu.make_async_copy(diag_hbm, blocks.at[0], load_sem.at[10])
    load_face = pltpu.make_async_copy(face_hbm, blocks.at[pl.ds(1, 6)], load_sem.at[11])
    for load in [*small, load_precond, *load_stash, load_diag, load_face]:
        load.start()

    lane = lax.broadcasted_iota(jnp.int32, (8, LANES), 1)
    sub = lax.broadcasted_iota(jnp.int32, (8, LANES), 0)
    left = lane < LANES // 2
    pair = 2 * (lane % (LANES // 2))

    def halos(step):
        return (
            pltpu.make_async_remote_copy(
                src_ref=rim_out.at[step, 0], dst_ref=rim_in.at[step, 0],
                send_sem=halo_send_sem.at[step, 0], recv_sem=halo_recv_sem.at[step, 0],
                device_id=(zone, rank + 1), device_id_type=MESH,
            ),
            pltpu.make_async_remote_copy(
                src_ref=rim_out.at[step, 1], dst_ref=rim_in.at[step, 1],
                send_sem=halo_send_sem.at[step, 1], recv_sem=halo_recv_sem.at[step, 1],
                device_id=(zone, rank - 1), device_id_type=MESH,
            ),
        )

    def start_halos(step):
        up, down = halos(step)
        for k in range(RIM_TILES):
            near_rows = slice(8 * k, 8 * k + 8)
            last, first = search[step, 1, near_rows, :], search[step, 0, near_rows, :]
            if RIM_TILES + k < TILES:
                far_rows = slice(8 * (RIM_TILES + k), 8 * (RIM_TILES + k) + 8)
                last = jnp.where(left, half_turn(search[step, 1, far_rows, :]), last)
                first = jnp.where(left, first, half_turn(search[step, 0, far_rows, :]))
            rim_out[step, 0, near_rows, :] = last
            rim_out[step, 1, near_rows, :] = first

        @pl.when(rank < RANKS - 1)
        def _():
            up.start()

        @pl.when(rank > 0)
        def _():
            down.start()

    def wait_halos(step):
        up, down = halos(step)

        @pl.when(rank > 0)
        def _():
            up.wait_recv()

        @pl.when(rank == 0)
        def _():
            rim_in[step, 0] = jnp.zeros((8 * RIM_TILES, LANES), F32)

        @pl.when(rank < RANKS - 1)
        def _():
            down.wait_recv()

        @pl.when(rank == RANKS - 1)
        def _():
            rim_in[step, 1] = jnp.zeros((8 * RIM_TILES, LANES), F32)

        @pl.when(rank < RANKS - 1)
        def _():
            up.wait_send()

        @pl.when(rank > 0)
        def _():
            down.wait_send()

    def rows_from(tiles):
        tiles = [
            jnp.where(sub < 4, one, two) + pltpu.roll(jnp.where(sub < 4, two, one), 4, 0)
            for one, two in zip(tiles[:4], tiles[4:])
        ]
        for shift in (2, 1):
            half = len(tiles) // 2
            tiles = [
                jnp.where(sub % (2 * shift) < shift, one + pltpu.roll(one, 8 - shift, 0), two + pltpu.roll(two, shift, 0))
                for one, two in zip(tiles[:half], tiles[half:])
            ]
        return tiles[0]

    def apply_precond(step):
        def rows_of(block, _):
            first = pl.multiple_of(block * 8, 8)
            for c in range(2):
                half = slice(c * LANES, c * LANES + LANES)
                vector = [near[0, t * 8 : t * 8 + 8, half] for t in range(TILES)]
                search[step, c, pl.ds(first, 8), :] = rows_from([
                    add_up(precond[first + i, t * 8 : t * 8 + 8, half] * vector[t] for t in range(TILES)) for i in range(8)
                ])
            return 0

        lax.fori_loop(0, TILES, rows_of, 0, unroll=TILES)

    def expand_counts(c):
        tile = jnp.broadcast_to(counts[...], (8, LANES))
        return gather_lanes(tile, c * 32 + lane // CAP)

    def gather_sending(step, c):
        at = jnp.broadcast_to(rows[pl.ds(c, 1), :], (8, LANES))
        live = jnp.where(lane % CAP < expand_counts(c), 1.0, 0.0)
        low, at = at < LANES, at % LANES
        for t in range(TILES):
            first = gather_lanes(search[step, 0, t * 8 : t * 8 + 8, :], at)
            second = gather_lanes(search[step, 1, t * 8 : t * 8 + 8, :], at)
            sending[c, t * 8 : t * 8 + 8, :] = jnp.where(low, first, second) * live

    def couple(pair_of):
        def step_of(i, acc):
            row = pl.multiple_of(i * B, 8)
            added = []
            for c in pair_of:
                factor = jnp.broadcast_to(sending[c, pl.ds(i, 1), :], (8, LANES))
                added += [stash[c, pl.ds(row + t * 8, 8), :] * factor for t in range(TILES)]
            return tuple(old + new for old, new in zip(acc, added))

        zero = jnp.zeros((8, LANES), F32)
        sums = lax.fori_loop(0, B, step_of, (zero,) * (2 * TILES), unroll=B)
        return sums[:TILES], sums[TILES:]

    def pack(step, p, couplings, scalars):
        zero = jnp.zeros((8, LANES), F32)
        tiles = []
        for h in range(2):
            for t in range(TILES):
                first = gather_lanes(couplings[0][t], pair + h)
                second = gather_lanes(couplings[1][t], pair + h)
                tiles.append(jnp.where(left, first, second))
            first = gather_lanes(jnp.broadcast_to(cols[pl.ds(2 * p, 1), :], (8, LANES)), pair + h)
            second = gather_lanes(jnp.broadcast_to(cols[pl.ds(2 * p + 1, 1), :], (8, LANES)), pair + h)
            extra = jnp.where(sub == 0, jnp.where(left, first, second).astype(F32), 0.0)
            for place_of, scalar in enumerate(scalars):
                extra = jnp.where(sub == 1 + place_of, scalar, extra)
            tiles += [extra, zero, zero]
        turned = jnp.concatenate(tiles, axis=0).T
        for d in range(64):
            send[step, 64 * p + d] = turned[2 * d : 2 * d + 2, :]

    def message(step, kind, offset):
        z, r = (zone + ahead[kind]) % 4, rank_at(offset)
        spot = offset[0] * 8 + offset[1] * 2 + offset[2]
        return pltpu.make_async_remote_copy(
            src_ref=send.at[step, z * RANKS + r], dst_ref=arrived.at[step, ahead[kind] * RANKS + spot],
            send_sem=send_sem.at[step], recv_sem=recv_sem.at[step],
            device_id=(z, r), device_id_type=MESH,
        )

    def own(step):
        return pltpu.make_async_copy(send.at[step, me], arrived.at[step, 0], own_sem.at[step])

    def all_arrived(step):
        others = arrived.at[step, pl.ds(1, DEVICES - 1)]
        pltpu.make_async_copy(others, others, recv_sem.at[step]).wait()
        own(step).wait()

    def prepare(step, k, scalars):
        pair_of = chunks[2 * k : 2 * k + 2]
        for j, c in enumerate(pair_of):
            if step == 0:
                load_stash[2 * k + j].wait()
            gather_sending(step, c)
        pack(step, pairs[k], couple(pair_of), scalars)

    def first_out(other):
        return other[0] > 0

    def post(step, first):
        for other in KINDS:
            if first_out(other) == first:
                message(step, *other).start()

    def apply_local(step):
        for t in range(TILES):
            tile = slice(t * 8, t * 8 + 8)
            zero_tile = search[step, 0, tile, :]
            one_tile = search[step, 1, tile, :]
            if t < RIM_TILES:
                rim_tile = jnp.where(left, rim_in[step, 1, tile, :], rim_in[step, 0, tile, :])
            else:
                packed = slice((t - RIM_TILES) * 8, (t - RIM_TILES) * 8 + 8)
                rim_tile = half_turn(jnp.where(left, rim_in[step, 0, packed, :], rim_in[step, 1, packed, :]))
            near[0, tile, :LANES] = zero_tile
            near[0, tile, LANES:] = one_tile
            for f in range(6):
                for c in range(2):
                    at = jnp.broadcast_to(nbrs[f : f + 1, c * LANES : c * LANES + LANES], (8, LANES))
                    index = (at + 64) % LANES
                    found = jnp.where(
                        (at >= 64) & (at < 192), gather_lanes(zero_tile, index),
                        jnp.where((at >= 192) & (at < 320), gather_lanes(one_tile, index), gather_lanes(rim_tile, index)),
                    )
                    near[1 + f, tile, c * LANES : c * LANES + LANES] = found
        if step == 0:
            load_diag.wait()
            load_face.wait()

        def rows_of(block, _):
            first = pl.multiple_of(block * 8, 8)
            for c in range(2):
                half = slice(c * LANES, c * LANES + LANES)
                sums = [None] * 8
                for b in range(7):
                    vector = [near[b, t * 8 : t * 8 + 8, half] for t in range(TILES)]
                    for i in range(8):
                        term = add_up(blocks[b, first + i, t * 8 : t * 8 + 8, half] * vector[t] for t in range(TILES))
                        sums[i] = term if b == 0 else sums[i] + term
                image[pl.ds(first, 8), half] = rows_from(sums)
            return 0

        lax.fori_loop(0, TILES, rows_of, 0)

    def received(step):
        return jnp.concatenate([arrived[step, k] for k in range(DEVICES)], axis=0)

    def sums_of(table):
        tile = add_up(table[8 * k : 8 * k + 8, :] for k in range(2 * DEVICES // 8))
        return jnp.sum(tile, axis=0, keepdims=True) * 0.5

    def scattered(table):
        turned = table.T
        halves = []
        for h in range(2):
            rest = turned[64 * h : 64 * h + 48, :]
            parts = []
            for _ in range(3):
                part = rest.astype(jnp.bfloat16)
                parts.append(part)
                rest = rest - part.astype(F32)
            halves.append(jnp.concatenate(parts, axis=0))
        product = jnp.dot(jnp.concatenate(halves, axis=1), onehot[...], preferred_element_type=F32)
        return product[:B] + product[48 : 48 + B] + product[96 : 96 + B]

    small[0].wait()
    near[0] = rhs[...] * DOWN
    square = total(rhs[...] * rhs[...])
    load_precond.wait()
    apply_precond(0)
    small[1].wait()
    small[2].wait()
    small[3].wait()
    small[4].wait()
    for k in range(2):
        prepare(0, k, (square,))
    pl.semaphore_wait(barrier, DEVICES - 1)
    post(0, True)
    start_halos(0)
    post(0, False)
    own(0).start()
    wait_halos(0)
    apply_local(0)
    all_arrived(0)
    table = received(0)
    element = lax.broadcasted_iota(jnp.int32, (256, 256), 1).astype(F32)
    for h in range(2):
        column = table[:, 64 * h + B : 64 * h + B + 1]
        onehot[256 * h : 256 * h + 256, :] = jnp.where(element == column, 1.0, 0.0).astype(jnp.bfloat16)
    sums = sums_of(table)
    square = sums[:, B + 1 : B + 2]
    beta = jnp.sqrt(square + EPS)
    shrunk = 1.0 / beta
    basis0 = rhs[...] * shrunk
    factor = UP * shrunk
    work0 = (image[...] + scattered(table)) * factor
    search0[:, :LANES] = search[0, 0] * factor
    search0[:, LANES:] = search[0, 1] * factor

    near[0] = work0
    apply_precond(1)
    scalars = (total(work0 * basis0), total(work0 * work0))
    prepare(1, 0, scalars)
    post(1, True)
    start_halos(1)
    prepare(1, 1, scalars)
    post(1, False)
    own(1).start()
    wait_halos(1)
    apply_local(1)
    all_arrived(1)
    table = received(1)
    sums = sums_of(table)
    h00 = sums[:, B + 1 : B + 2]
    shrink = 1.0 / jnp.sqrt(sums[:, B + 2 : B + 3] + EPS)
    unit = square / (square + EPS)
    work1 = work0 - h00 * basis0
    second = (image[...] + scattered(table) - h00 * work0) * shrink

    values = (
        total(work1 * work1), total(work1 * basis0), total(second * basis0), total(second * work1), total(second * second)
    )
    row_lane = lax.broadcasted_iota(jnp.int32, (1, LANES), 1)
    mine = jnp.zeros((1, LANES), F32)
    for place_of, value in enumerate(values):
        mine = jnp.where(row_lane == place_of, value, mine)
    dots[...] = mine
    dots_in[0] = mine

    def tell(other):
        dz, (dy, dx, dc) = other
        return pltpu.make_async_remote_copy(
            src_ref=dots, dst_ref=dots_in.at[dz * RANKS + dy * 8 + dx * 2 + dc],
            send_sem=send_sem.at[2], recv_sem=recv_sem.at[2],
            device_id=place(other), device_id_type=MESH,
        )

    for other in OTHERS:
        tell(other).start()
    others = dots_in.at[pl.ds(1, DEVICES - 1)]
    pltpu.make_async_copy(others, others, recv_sem.at[2]).wait()
    sums = add_up(dots_in[k] for k in range(DEVICES))
    n1, cross, a, b, d = (sums[:, k : k + 1] for k in range(5))
    n1_eps = n1 + EPS
    across = b - a * cross
    along = across / n1_eps
    left_over = d - 2.0 * a * a + unit * a * a - 2.0 * along * b + along * along * n1 + 2.0 * a * along * cross
    n00 = h00 * h00 + n1_eps
    mixed = h00 * a + across
    lower = mixed / n00
    corner = a * a + along * across + (jnp.maximum(left_over, 0.0) + EPS * n1_eps * shrink * shrink)
    y1 = beta * (a - lower * h00) / (corner - lower * mixed)
    c0 = (beta * h00 - mixed * y1) / n00
    y1_small = y1 * shrink
    own_part = c0 - y1_small * h00
    for c in range(2):
        half = slice(c * LANES, c * LANES + LANES)
        out_ref[0, :, half] = own_part * search0[:, half] + y1_small * search[1, c]
    out_ref[1] = rhs[...] - c0 * work0 - y1 * second

    for step in range(2):
        others = arrived.at[step, pl.ds(1, DEVICES - 1)]
        pltpu.make_async_copy(others, others, send_sem.at[step]).wait()
    others = dots_in.at[pl.ds(1, DEVICES - 1)]
    pltpu.make_async_copy(others, others, send_sem.at[2]).wait()


def per_device(rhs, diag, precond, face, nbrs, stash, rows, cols, counts):
    arrays = (
        rhs, diag, precond, face, nbrs, stash, rows.reshape(4, LANES), cols.reshape(4, LANES), counts.reshape(1, LANES)
    )
    anywhere = pl.BlockSpec(memory_space=pl.ANY)
    out = pl.pallas_call(
        kernel,
        out_shape=jax.ShapeDtypeStruct((2, B, 256), F32),
        in_specs=[anywhere] * 9,
        out_specs=pl.BlockSpec(memory_space=pltpu.VMEM),
        scratch_shapes=[
            pltpu.VMEM((B, 256), F32),
            pltpu.VMEM((B, B, 256), F32),
            pltpu.VMEM((7, B, B, 256), F32),
            pltpu.VMEM((4, B * B, LANES), F32),
            pltpu.VMEM((6, 256), jnp.int32),
            pltpu.VMEM((4, LANES), jnp.int32),
            pltpu.VMEM((4, LANES), jnp.int32),
            pltpu.VMEM((1, LANES), jnp.int32),
            pltpu.VMEM((7, B, 256), F32),
            pltpu.VMEM((2, 2, B, LANES), F32),
            pltpu.VMEM((2, 2, 8 * RIM_TILES, LANES), F32),
            pltpu.VMEM((2, 2, 8 * RIM_TILES, LANES), F32),
            pltpu.VMEM((B, 256), F32),
            pltpu.VMEM((B, 256), F32),
            pltpu.VMEM((4, B, LANES), F32),
            pltpu.VMEM((2, DEVICES, 2, LANES), F32),
            pltpu.VMEM((2, DEVICES, 2, LANES), F32),
            pltpu.VMEM((512, 256), jnp.bfloat16),
            pltpu.VMEM((1, LANES), F32),
            pltpu.VMEM((DEVICES, 1, LANES), F32),
            pltpu.SemaphoreType.DMA((12,)),
            pltpu.SemaphoreType.DMA((2,)),
            pltpu.SemaphoreType.DMA((3,)),
            pltpu.SemaphoreType.DMA((3,)),
            pltpu.SemaphoreType.DMA((2, 2)),
            pltpu.SemaphoreType.DMA((2, 2)),
        ],
        compiler_params=pltpu.CompilerParams(
            collective_id=0, has_side_effects=True, vmem_limit_bytes=48 * 2**20
        ),
        name="gmres",
    )(*(pltpu.with_memory_space_constraint(array, pltpu.HBM) for array in arrays))
    return out[0], out[1]


def solution(mesh):
    spread = ("zone", "rank")
    return jax.shard_map(
        per_device,
        mesh=mesh,
        in_specs=(
            P(None, spread),
            P(None, None, spread),
            P(None, None, spread),
            P(None, None, None, spread),
            P(None, spread),
            P(None, spread),
            P(spread),
            P(spread),
            P(spread),
        ),
        out_specs=(P(None, spread), P(None, spread)),
        check_vma=False,
    )
```
